256 devices in a mesh: group: 64 (over y_hi, z, x), tensor: 4 (over y_lo, core).
Axes of the slice: x: 4, y: 4 (y_hi: 2, y_lo: 2; y = y_hi * 2 + y_lo), z: 8, core: 2. Of those that a mesh axis runs over, the one named last changes fastest.
Arguments:
- hidden: bfloat16 [2, 1024, 4096], P(None, 'group'), may hold values from -6 to 6
- queries: bfloat16 [2, 1024, 32, 128], P(None, 'group', 'tensor'), may hold values from -4.5 to 4.5
- kv_cache: bfloat16 [2, 1024, 4, 256, 128], P(None, 'group', 'tensor'), may hold values from -4.5 to 4.5
- lengths: int32 [1024], P('group'), may hold values from 2 to 256, as said below
- frozen_key_value: bfloat16 [4096, 2, 512], P(None, None, 'tensor'), may hold values from -0.09375 to 0.09375
- frozen_output_weight: bfloat16 [4096, 4096], P('tensor'), may hold values from -0.09375 to 0.09375
- down_kv: bfloat16 [4096, 2, 32], P('group'), may hold values from -0.09375 to 0.09375
- up_kv: bfloat16 [2, 32, 4, 128], P(None, None, 'tensor', 'group'), may hold values from -1 to 1
- down_o: bfloat16 [32, 128, 32], P('tensor', 'group'), may hold values from -0.09375 to 0.09375
- up_o: bfloat16 [32, 4096], P(None, 'group'), may hold values from -1 to 1
Outputs:
- attended: bfloat16 [2, 1024, 4096], P(None, 'group')
- new_kv: bfloat16 [2, 2, 1024, 4, 128], P(None, None, 'group', 'tensor')
The draws below stay inside these ranges and needn't reach their ends.
Inputs may be any that keep to these rules, and one draw needn't show every extreme that they name: `lengths`: at least one row has exactly 256.
All inputs are finite; a program needn't handle non-finite values.
Results may differ from the reference program's by a relative error of at most 0.0083.
Values may be sent and summed in bfloat16 or wider, within the bound.
A program may use at most 64 MiB of HBM per device.

```python
import math
import jax
import jax.numpy as jnp
from jax import lax

D = 4096
HEADS = 32
KV_HEADS = 4
HEAD = 128
RANK = 32
STEPS = 2
CACHE = 256
ROWS = 1024


def draw_kv_cache(key, part):
    key = jax.random.fold_in(key, 11)
    shape = (2, ROWS, KV_HEADS, CACHE, HEAD)
    values = jnp.clip(jax.random.normal(key, shape, jnp.float32), -4.5, 4.5)
    return values.astype(jnp.bfloat16)


def draw_queries(key, part):
    key = jax.random.fold_in(key, 12)
    shape = (STEPS, ROWS, HEADS, HEAD)
    values = jnp.clip(jax.random.normal(key, shape, jnp.float32), -4.5, 4.5)
    return values.astype(jnp.bfloat16)


def draw_lengths(key, part):
    key = jax.random.fold_in(key, 13)
    first, second = jax.random.split(key)
    drawn = jax.random.randint(first, (ROWS,), 2, CACHE + 1)
    chosen = jax.random.randint(second, (), 0, ROWS)
    return jnp.where(jnp.arange(ROWS) == chosen, CACHE, drawn).astype(jnp.int32)


def block_levels(rng, dims, shards, smallest, top_value):
    gain, own = 1.0, jax.random.fold_in(rng, 6)
    for position, blocks in shards:
        heights = jnp.exp(jax.random.uniform(jax.random.fold_in(own, position), (blocks,), jnp.float32, smallest / len(shards), top_value / len(shards)))
        gain = gain * jnp.repeat(heights, dims[position] // blocks).reshape([-1 if axis == position else 1 for axis in range(len(dims))])
    return gain


def scatter_about(rng, dims, deviation, most, cuts=(), kind=jnp.bfloat16):
    values = jax.random.normal(rng, dims, jnp.float32) * deviation
    if len(cuts) > 0:
        values = block_levels(rng, dims, cuts, -0.22, 0.18) * values
    return jnp.clip(values, min=-most, max=most).astype(kind)


def setup_inputs(seed: int = 0) -> dict:
    splits = jax.random.split(jax.random.key(seed), 11)
    return {
        "hidden": scatter_about(splits[0], (STEPS, ROWS, D), 1.0, 6.0, ((1, 64),)),
        "queries": draw_queries(jax.random.fold_in(splits[10], 71), 0),
        "kv_cache": draw_kv_cache(jax.random.fold_in(splits[10], 71), 0),
        "lengths": draw_lengths(jax.random.fold_in(splits[10], 71), 0),
        "frozen_key_value": scatter_about(splits[4], (D, 2, KV_HEADS * HEAD), D ** -0.5, 0.09375, ((2, 4),)),
        "frozen_output_weight": scatter_about(splits[5], (HEADS * HEAD, D), (HEADS * HEAD) ** -0.5, 0.09375, ((0, 4),)),
        "down_kv": scatter_about(splits[6], (D, 2, RANK), D ** -0.5, 0.09375, ((0, 64),)),
        "up_kv": scatter_about(splits[7], (2, RANK, KV_HEADS, HEAD), RANK ** -0.5, 1.0, ((2, 4), (3, 64))),
        "down_o": scatter_about(splits[8], (HEADS, HEAD, RANK), (HEADS * HEAD) ** -0.5, 0.09375, ((0, 4), (1, 64))),
        "up_o": scatter_about(splits[9], (RANK, D), RANK ** -0.5, 1.0, ((1, 64),)),
    }


ADAPTER_SCALE = 2.0
ROPE_BASE = 500000.0

def rotate(keys, positions):
    half = keys.shape[-1] // 2
    counter = jnp.arange(half, dtype=jnp.float32)
    inverse = jnp.exp(counter * (-2.0 * math.log(ROPE_BASE) / keys.shape[-1]))
    angle = positions.astype(jnp.float32)[:, None, None] * inverse
    cosine = jnp.cos(angle)
    sine = jnp.sin(angle)
    first = keys[..., :half]
    second = keys[..., half:]
    return jnp.concatenate([first * cosine - second * sine, second * cosine + first * sine], axis=-1)

def attend(query, keys, values, valid):
    scores = jnp.einsum('rkgd,rkpd->rkgp', query.astype(jnp.float32), keys.astype(jnp.float32))
    scores = scores * (1.0 / math.sqrt(query.shape[-1]))
    scores = jnp.where(valid[:, None, None, :], scores, -1e+30)
    top = lax.optimization_barrier(jnp.max(scores, axis=-1, keepdims=True))
    expo = jnp.exp(scores - top)
    weights = (expo / lax.optimization_barrier(jnp.sum(expo, axis=-1, keepdims=True))).astype(jnp.bfloat16)
    context = jnp.einsum('rkgp,rkpd->rkgd', weights.astype(jnp.float32), values.astype(jnp.float32))
    return context.astype(jnp.bfloat16)

def reference(hidden, queries, kv_cache, lengths, frozen_key_value, frozen_output_weight, down_kv, up_kv, down_o, up_o):
    rows = hidden.shape[1]
    kv_width = frozen_key_value.shape[2]
    up_kv_mat = up_kv.reshape(2, RANK, kv_width).astype(jnp.float32)
    key_value_update = jnp.einsum('dgr,grk->dgk', down_kv.astype(jnp.float32), up_kv_mat, precision=lax.Precision.HIGHEST)
    merged_key_value = (frozen_key_value.astype(jnp.float32) + ADAPTER_SCALE * key_value_update).astype(jnp.bfloat16)
    down_o_mat = down_o.reshape(HEADS * HEAD, RANK)
    output_update = jnp.dot(down_o_mat, up_o, preferred_element_type=jnp.float32)
    merged_output_weight = (frozen_output_weight.astype(jnp.float32) + ADAPTER_SCALE * output_update).astype(jnp.bfloat16)
    slots = lax.broadcasted_iota(jnp.int32, (rows, CACHE), 1)
    valid_cache = slots < lengths[:, None]
    new_keys = []
    new_values = []
    outputs = []
    written = []
    for step in range(STEPS):
        projected = jnp.dot(hidden[step], merged_key_value.reshape(D, 2 * kv_width), preferred_element_type=jnp.float32)
        projected = projected.reshape(rows, 2, KV_HEADS, HEAD)
        fresh_key = rotate(projected[:, 0], lengths + step).astype(jnp.bfloat16)
        fresh_value = projected[:, 1].astype(jnp.bfloat16)
        new_keys.append(fresh_key)
        new_values.append(fresh_value)
        keys = jnp.concatenate([kv_cache[0], jnp.stack(new_keys, axis=2)], axis=2)
        values = jnp.concatenate([kv_cache[1], jnp.stack(new_values, axis=2)], axis=2)
        valid = jnp.concatenate([valid_cache, jnp.ones((rows, step + 1), dtype=bool)], axis=1)
        query = queries[step].reshape(rows, KV_HEADS, HEADS // KV_HEADS, HEAD)
        context = attend(query, keys, values, valid).reshape(rows, HEADS * HEAD)
        outputs.append(jnp.dot(context, merged_output_weight, preferred_element_type=jnp.float32).astype(jnp.bfloat16))
        written.append(jnp.stack([fresh_key, fresh_value], axis=0))
    return (jnp.stack(outputs), jnp.stack(written))
```

```python
import math

import jax
import jax.numpy as jnp
from jax import lax
from jax.experimental import pallas as pl
from jax.experimental.pallas import tpu as pltpu
from jax.sharding import PartitionSpec as P

BF = jnp.bfloat16
F32 = jnp.float32
MESH = pl.DeviceIdType.MESH

ADAPTER_SCALE = 2.0
ROPE_BASE = 500000.0
SCALE = 1.0 / math.sqrt(128.0)
MASKED = -1e30

NT = (((1,), (1,)), ((), ()))


def dot(a, b):
    return jnp.dot(a, b, preferred_element_type=F32)


def dot_nt(a, b):
    return lax.dot_general(a, b, NT, preferred_element_type=F32)


def place(rows, columns, offset):
    i = lax.broadcasted_iota(jnp.int32, (rows, columns), 0)
    j = lax.broadcasted_iota(jnp.int32, (rows, columns), 1)
    return jnp.where(j == i + offset, 1.0, 0.0).astype(BF)


def kernel(
    hid_hbm, q_hbm, kv_hbm, len_ref, fkv_hbm, w_hbm, dkv_hbm, ukv_hbm, do_hbm, uo_hbm,
    att_hbm, nkv_hbm,
    hid, q_v, kv, fkv, w, dk_v, uk_v, do_v, uo_v,
    hx, qs, ga, gb, gt, gf, dmf, s16, s4,
    zs, zr, zos, zor, acc, mm, ll, ctxs, ctx, u,
    ps, pr, ys, yr, fs, nk, nv, nst, base,
    lsem, a1s, a1r, a2s, a2r, b1s, b1r, b2s, b2r, ts, tr, os, orr, pss, prs, yss, yrs, fss, frs, outs,
):
    g = lax.axis_index("group")
    t = lax.axis_index("tensor")
    yh = lax.div(g, 32)
    z = lax.rem(lax.div(g, 4), 8)
    x = lax.rem(g, 4)
    yl = lax.div(t, 2)
    c = lax.rem(t, 2)

    def group_of(yh_, z_, x_):
        return yh_ * 32 + z_ * 4 + x_

    def tensor_of(k):
        yl_ = yl if k < 2 else 1 - yl
        c_ = c if k % 2 == 0 else 1 - c
        return yl_ * 2 + c_

    def remote(src, dst, ss, rs, group, tensor):
        return pltpu.make_async_remote_copy(
            src_ref=src, dst_ref=dst, send_sem=ss, recv_sem=rs,
            device_id={"group": group, "tensor": tensor}, device_id_type=MESH,
        )

    def load(src, dst, i):
        copy = pltpu.make_async_copy(src, dst, lsem.at[i])
        copy.start()
        return copy

    l_dk = load(dkv_hbm.at[pl.ds(pl.multiple_of(t * 16, 16), 16), :], dk_v, 0)
    l_uk = load(ukv_hbm, uk_v, 1)
    l_do = load(do_hbm, do_v, 2)
    l_uo = load(uo_hbm, uo_v, 3)
    l_hid = load(hid_hbm, hid, 4)
    l_q = load(q_hbm, q_v, 5)
    l_fkv = load(fkv_hbm, fkv, 6)
    l_kv = load(kv_hbm, kv, 7)
    l_w = load(w_hbm, w, 8)

    barrier = pltpu.get_barrier_semaphore()

    def xy_peer(k):
        return (yh if k < 4 else 1 - yh), lax.rem(x + k % 4, 4)

    for k in range(1, 8):
        pl.semaphore_signal(barrier, inc=1, device_id={"group": group_of(yh, lax.rem(z + k, 8), x), "tensor": t}, device_id_type=MESH)
    for k in range(1, 8):
        yh_, x_ = xy_peer(k)
        pl.semaphore_signal(barrier, inc=1, device_id={"group": group_of(yh_, z, x_), "tensor": t}, device_id_type=MESH)
    for k in range(1, 4):
        pl.semaphore_signal(barrier, inc=1, device_id={"group": g, "tensor": tensor_of(k)}, device_id_type=MESH)

    s4[...] = jnp.zeros_like(s4)
    l_dk.wait()
    l_uk.wait()
    l_do.wait()
    for h in range(8):
        s16[2 * h : 2 * h + 2, :] = do_v[h].astype(F32)
    for k in range(2):
        s4[2 * k : 2 * k + 2, :] = uk_v[k].astype(F32)
    package = (
        dot(dk_v[...], place(64, 128, 0))
        + dot(s16[...].astype(BF), place(32, 128, 64))
        + dot(s4[...].astype(BF), place(32, 128, 96))
    )
    ga[yh, z, x] = package.astype(BF)
    l_uo.wait()
    b_source = jnp.logical_and(yh == c, lax.div(z, 4) == yl)

    @pl.when(b_source)
    def _():
        up = uo_v[...]
        gb[lax.rem(z, 4), x] = (dot(up[0:16], place(64, 128, 0)) + dot(up[16:32], place(64, 128, 64))).astype(BF)

    pl.semaphore_wait(barrier, 17)

    a1 = []
    for k in (4, 3, 5, 2, 6, 1, 7):
        copy = remote(ga.at[yh, z, x], ga.at[yh, z, x], a1s.at[k], a1r.at[k], group_of(yh, lax.rem(z + k, 8), x), t)
        copy.start()
        a1.append(copy)
    zz_mine = lax.rem(z, 4)

    def b1_copy(k):
        return remote(gb.at[zz_mine, x], gb.at[zz_mine, x], b1s.at[k], b1r.at[zz_mine], group_of(yh, lax.rem(z + k, 8), x), t)

    @pl.when(b_source)
    def _():
        for k in (4, 3, 5, 2, 6, 1, 7):
            b1_copy(k).start()

    l_hid.wait()
    row = lax.broadcasted_iota(jnp.int32, (128, 512), 0)
    col = lax.broadcasted_iota(jnp.int32, (128, 512), 1)
    spread = jnp.where(jnp.where(col < 256, col, col - 257) == 2 * row, 1.0, 0.0).astype(BF)

    def spread_chunk(a, _):
        part = dot(hid[:, pl.ds(pl.multiple_of(a * 128, 128), 128)], spread).astype(BF)
        at = pl.ds(pl.multiple_of(a * 256, 256), 256)
        hx[0:32, at] = part[:, :256]
        hx[32:64, at] = part[:, 256:]
        return 0

    lax.fori_loop(0, 32, spread_chunk, 0, unroll=8)

    for copy in a1:
        copy.wait_recv()
    a2 = []
    for k in (6, 2, 5, 7, 4, 1, 3):
        yh_, x_ = xy_peer(k)
        copy = remote(ga.at[yh, :, x], ga.at[yh, :, x], a2s.at[k], a2r.at[k], group_of(yh_, z, x_), t)
        copy.start()
        a2.append(copy)

    def b2_copy(k):
        yh_, x_ = xy_peer(k)
        return remote(gb.at[:, x], gb.at[:, x], b2s.at[k], b2r.at[k], group_of(yh_, z, x_), t)

    @pl.when(yh == c)
    def _():
        for zz in range(4):
            @pl.when(yl * 4 + zz != z)
            def _():
                remote(gb.at[zz, x], gb.at[zz, x], b1s.at[0], b1r.at[zz], g, t).wait_recv()
        for k in (6, 2, 5, 7, 4, 1, 3):
            b2_copy(k).start()

    l_fkv.wait()

    def project(a, total):
        at = pl.ds(pl.multiple_of(a * 1024, 1024), 1024)
        return total + dot(hx[:, at], fkv[at, :])

    base[...] = lax.fori_loop(0, 8, project, jnp.zeros((64, 128), F32), unroll=4)

    sub = lax.broadcasted_iota(jnp.int32, (32, 128), 0)
    lane = lax.broadcasted_iota(jnp.int32, (32, 128), 1)
    later = jnp.where(sub >= 16, 1, 0)
    in_step = sub - 16 * later
    position = later
    for r in range(16):
        position = position + jnp.where(in_step == r, len_ref[r], 0)
    counter = jnp.where(lane < 64, lane, lane - 64).astype(F32)
    angle = position.astype(F32) * jnp.exp(counter * (-2.0 * math.log(ROPE_BASE) / 128))
    cosine = jnp.cos(angle)
    sine = jnp.sin(angle)
    sine = jnp.where(lane < 64, -sine, sine)

    l_q.wait()
    for s in range(2):
        qs[:, s * 8 : s * 8 + 8, :] = q_v[s].astype(F32)
    l_kv.wait()
    slots = lax.broadcasted_iota(jnp.int32, (16, 256), 1)

    def cached(r, _):
        scores = dot_nt(qs[r].astype(BF), kv[r]) * SCALE
        scores = jnp.where(slots < len_ref[r], scores, MASKED)
        top = jnp.max(scores, axis=1, keepdims=True)
        expo = jnp.exp(scores - top)
        acc[r] = dot(expo.astype(BF), kv[16 + r])
        mm[r] = jnp.broadcast_to(top, (16, 128))
        ll[r] = jnp.broadcast_to(jnp.sum(expo, axis=1, keepdims=True), (16, 128))
        return 0

    lax.fori_loop(0, 16, cached, 0, unroll=8)
    u[...] = jnp.zeros_like(u)

    for copy in a2:
        copy.wait_recv()
    for y_ in range(2):
        for z_ in range(8):
            first = (y_ * 8 + z_) * 64
            gf[first : first + 64, :] = ga[y_, z_].astype(F32).reshape(64, 128)
    lane16 = lax.broadcasted_iota(jnp.int32, (16, 128), 1)

    def down_chunk(a, _):
        even = gf[pl.ds(pl.multiple_of(a * 32, 32), 16), :]
        odd = gf[pl.ds(pl.multiple_of(a * 32 + 16, 16), 16), :]
        gt[:, pl.ds(pl.multiple_of(a * 128, 128), 128)] = jnp.where(lane16 < 64, even, pltpu.roll(odd, 64, 1)).astype(BF)
        return 0

    lax.fori_loop(0, 32, down_chunk, 0, unroll=8)
    low = dot_nt(hid[...], gt[...]).astype(BF)
    zs[...] = dot(low, place(16, 128, 96 + 16 * c)).astype(BF)
    t1 = []
    for k in (2, 3, 1):
        copy = remote(zs, zr.at[k], ts.at[k], tr.at[k], g, tensor_of(k))
        copy.start()
        t1.append(copy)

    for j in range(16):
        dmf[pl.ds((j // 2) * 128 + j % 2, 64, stride=2), :] = gf[pl.ds(j, 64, stride=16), :]

    for copy in t1:
        copy.wait_recv()
    mine = (zs[...].astype(F32) + zr[1].astype(F32)).astype(BF)
    theirs = (zr[2].astype(F32) + zr[3].astype(F32)).astype(BF)
    is_key = (yl == 0).astype(F32)
    z_key = (mine.astype(F32) * is_key + theirs.astype(F32) * (1.0 - is_key)).astype(BF)
    z_value = (mine.astype(F32) * (1.0 - is_key) + theirs.astype(F32) * is_key).astype(BF)
    key = base[0:32, :] + ADAPTER_SCALE * dot_nt(z_key, dmf[0:128, :].astype(BF))
    value = base[32:64, :] + ADAPTER_SCALE * dot_nt(z_value, dmf[128:256, :].astype(BF))
    key = (key * cosine + pltpu.roll(key, 64, 1) * sine).astype(BF)
    value = value.astype(BF)
    nk[...] = key.astype(F32)
    nv[...] = value.astype(F32)
    for s in range(2):
        nst[s, 0] = key[s * 16 : s * 16 + 16]
        nst[s, 1] = value[s * 16 : s * 16 + 16]
    l_nkv = pltpu.make_async_copy(nst, nkv_hbm, outs.at[4])
    l_nkv.start()

    first_step = lax.broadcasted_iota(jnp.int32, (16, 128), 0) < 8
    for r in range(16):
        query = qs[r]
        s0 = jnp.sum(query * nk[r : r + 1, :], axis=1, keepdims=True) * SCALE
        s1 = jnp.sum(query * nk[16 + r : 17 + r, :], axis=1, keepdims=True) * SCALE
        s0 = jnp.broadcast_to(s0, (16, 128))
        s1 = jnp.where(first_step, MASKED, jnp.broadcast_to(s1, (16, 128)))
        top = jnp.maximum(mm[r], jnp.maximum(s0, s1))
        alpha = jnp.exp(mm[r] - top)
        p0 = jnp.exp(s0 - top)
        p1 = jnp.exp(s1 - top)
        total = alpha * ll[r] + p0 + p1
        ctxs[r * 16 : r * 16 + 16, :] = (alpha * acc[r] + p0 * nv[r : r + 1, :] + p1 * nv[16 + r : 17 + r, :]) / total
    for s in range(2):
        for h in range(8):
            ctx[s * 16 : s * 16 + 16, h * 128 : h * 128 + 128] = ctxs[pl.ds(s * 8 + h, 16, stride=16), :].astype(BF)

    context = ctx[...]
    zos[...] = dot(context, dmf[...].astype(BF))
    t2 = []
    for k in (2, 3, 1):
        copy = remote(zos, zor.at[k], os.at[k], orr.at[k], g, tensor_of(k))
        copy.start()
        t2.append(copy)

    @pl.when(yh == c)
    def _():
        for k in range(1, 4):
            b2_copy(k).wait_recv()

    @pl.when(yh != c)
    def _():
        for k in range(4, 8):
            b2_copy(k).wait_recv()

    for a in range(8):
        even = gb[a // 2, 2 * (a % 2)].astype(F32)
        odd = gb[a // 2, 2 * (a % 2) + 1].astype(F32)
        at = pl.ds(pl.multiple_of(yl * 1024 + a * 128, 128), 128)
        u[64:80, at] = jnp.where(lane16 < 64, even, pltpu.roll(odd, 64, 1)).astype(BF)
        u[80:96, at] = jnp.where(lane16 < 64, pltpu.roll(even, 64, 1), odd).astype(BF)

    l_w.wait()
    core_peer = tensor_of(1)
    chip_peer = tensor_of(2)

    def columns(half, j):
        return pl.ds(pl.multiple_of(half * 2048 + j * 512, 512), 512)

    def give_copy(j):
        return remote(ps.at[j], pr.at[j], pss.at[j], prs.at[j], g, core_peer)

    def chip_copy(j):
        return remote(ys.at[j], yr.at[j], yss.at[j], yrs.at[j], g, chip_peer)

    def final_copy(j):
        return remote(fs.at[j], att_hbm.at[:, columns(c, j)], fss.at[j], frs.at[j], g, core_peer)

    def local_copy(j):
        return pltpu.make_async_copy(fs.at[j], att_hbm.at[:, columns(c, j)], outs.at[j])

    def give(j):
        ps[j] = dot(context, w[:, columns(1 - c, j)]).astype(BF)
        give_copy(j).start()

    def keep(j, low_sum):
        part = dot(context, w[:, columns(c, j)]) + dot(low_sum, u[:, j * 512 : j * 512 + 512])
        give_copy(j).wait_recv()
        ys[j] = (part + pr[j].astype(F32)).astype(BF)
        chip_copy(j).start()

    def finish(j):
        chip_copy(j).wait_recv()
        fs[j] = (ys[j].astype(F32) + yr[j].astype(F32)).astype(BF)
        final_copy(j).start()
        local_copy(j).start()

    give(0)
    give(1)
    for copy in t2:
        copy.wait_recv()
    low_sum = (zos[...] + zor[1]) + (zor[2] + zor[3])
    low_sum = jnp.where(jnp.logical_and(lane >= 64, lane < 96), ADAPTER_SCALE * low_sum, 0.0).astype(BF)
    keep(0, low_sum)
    give(2)
    keep(1, low_sum)
    give(3)
    keep(2, low_sum)
    finish(0)
    keep(3, low_sum)
    finish(1)
    finish(2)
    finish(3)

    for copy in a1 + a2 + t1 + t2:
        copy.wait_send()

    @pl.when(b_source)
    def _():
        for k in range(1, 8):
            b1_copy(k).wait_send()

    @pl.when(yh == c)
    def _():
        for k in range(1, 8):
            b2_copy(k).wait_send()

    l_nkv.wait()
    for j in range(4):
        give_copy(j).wait_send()
        chip_copy(j).wait_send()
        local_copy(j).wait()
        final_copy(j).wait()


def local(hidden, queries, kv_cache, lengths, frozen_key_value, frozen_output_weight, down_kv, up_kv, down_o, up_o):
    hbm = pl.BlockSpec(memory_space=pltpu.HBM)
    dma = pltpu.SemaphoreType.DMA
    args = (
        hidden.reshape(32, 4096),
        queries,
        kv_cache.reshape(32, 256, 128),
        lengths,
        frozen_key_value.reshape(8192, 128),
        frozen_output_weight,
        down_kv.transpose(1, 2, 0).reshape(64, 64),
        up_kv.transpose(0, 2, 3, 1).reshape(2, 2, 32),
        down_o,
        up_o,
    )
    v = pltpu.VMEM
    attended, new_kv = pl.pallas_call(
        kernel,
        out_shape=(
            jax.ShapeDtypeStruct((32, 4096), BF),
            jax.ShapeDtypeStruct((2, 2, 16, 128), BF),
        ),
        in_specs=[hbm, hbm, hbm, pl.BlockSpec(memory_space=pltpu.SMEM)] + [hbm] * 6,
        out_specs=(hbm, hbm),
        scratch_shapes=[
            v((32, 4096), BF), v((2, 16, 8, 128), BF), v((32, 256, 128), BF), v((8192, 128), BF), v((1024, 4096), BF),
            v((16, 64), BF), v((2, 2, 32), BF), v((8, 2, 32), BF), v((32, 64), BF),
            v((64, 8192), BF), v((16, 16, 128), F32), v((2, 8, 4, 16, 128), BF), v((4, 4, 16, 128), BF),
            v((16, 4096), BF), v((1024, 128), F32), v((1024, 128), F32), v((16, 32), F32), v((16, 32), F32),
            v((32, 128), BF), v((4, 32, 128), BF), v((32, 128), F32), v((4, 32, 128), F32),
            v((16, 16, 128), F32), v((16, 16, 128), F32), v((16, 16, 128), F32), v((256, 128), F32),
            v((32, 1024), BF), v((128, 2048), BF),
            v((4, 32, 512), BF), v((4, 32, 512), BF), v((4, 32, 512), BF), v((4, 32, 512), BF), v((4, 32, 512), BF),
            v((32, 128), F32), v((32, 128), F32), v((2, 2, 16, 128), BF), v((64, 128), F32),
            dma((9,)), dma((8,)), dma((8,)), dma((8,)), dma((8,)), dma((8,)), dma((4,)), dma((8,)), dma((8,)),
            dma((4,)), dma((4,)), dma((4,)), dma((4,)), dma((4,)), dma((4,)), dma((4,)), dma((4,)), dma((4,)), dma((4,)),
            dma((5,)),
        ],
        compiler_params=pltpu.CompilerParams(
            collective_id=0, has_side_effects=True, vmem_limit_bytes=48 * 1024 * 1024
        ),
    )(*args)
    return attended.reshape(2, 16, 4096), new_kv.reshape(2, 2, 16, 1, 128)


def solution(mesh):
    placed = (
        P(None, "group", None),
        P(None, "group", "tensor", None),
        P(None, "group", "tensor", None, None),
        P("group"),
        P(None, None, "tensor"),
        P("tensor", None),
        P("group", None, None),
        P(None, None, "tensor", "group"),
        P("tensor", "group", None),
        P(None, "group"),
    )
    return jax.shard_map(
        local,
        mesh=mesh,
        in_specs=placed,
        out_specs=(P(None, "group", None), P(None, None, "group", "tensor", None)),
        check_vma=False,
    )
```

```python
import math

import jax
import jax.numpy as jnp
from jax import lax
from jax.experimental import pallas as pl
from jax.experimental.pallas import tpu as pltpu
from jax.sharding import PartitionSpec as P

BF = jnp.bfloat16
F32 = jnp.float32
MESH = pl.DeviceIdType.MESH

ADAPTER_SCALE = 2.0
ROPE_BASE = 500000.0
SCALE = 1.0 / math.sqrt(128.0)
MASKED = -1e30

NT = (((1,), (1,)), ((), ()))


def dot(a, b):
    return jnp.dot(a, b, preferred_element_type=F32)


def dot_nt(a, b):
    return lax.dot_general(a, b, NT, preferred_element_type=F32)


def place(rows, columns, offset):
    i = lax.broadcasted_iota(jnp.int32, (rows, columns), 0)
    j = lax.broadcasted_iota(jnp.int32, (rows, columns), 1)
    return jnp.where(j == i + offset, 1.0, 0.0).astype(BF)


def kernel(
    hid_hbm, q_hbm, kv_hbm, len_hbm, fkv_hbm, w_hbm, dkv_hbm, ukv_hbm, do_hbm, uo_hbm,
    att_hbm, nkv_hbm,
    hid, q_v, kv, fkv, w, dk_v, uk_v, do_v, uo_v,
    hx, qs, ga, gb, gt, gf, dmf, s16, s4,
    zs, zr, zos, zor, acc, mm, ll, ctxs, ctx, u,
    ps, pr, ys, yr, fs, nk, nv, nst, base, len_ref,
    lsem, one, prs, yrs,
):
    a1s, a1r, a2s, a2r, b1s, b1r, b2s, b2r, ts, tr, os, orr, pss, yss, fss, frs, outs, outk = (one.at[i] for i in range(18))
    g = lax.axis_index("group")
    t = lax.axis_index("tensor")
    yh = lax.div(g, 32)
    z = lax.rem(lax.div(g, 4), 8)
    x = lax.rem(g, 4)
    yl = lax.div(t, 2)
    c = lax.rem(t, 2)

    def group_of(yh_, z_, x_):
        return yh_ * 32 + z_ * 4 + x_

    def tensor_of(k):
        yl_ = yl if k < 2 else 1 - yl
        c_ = c if k % 2 == 0 else 1 - c
        return yl_ * 2 + c_

    def remote(src, dst, ss, rs, group, tensor):
        return pltpu.make_async_remote_copy(
            src_ref=src, dst_ref=dst, send_sem=ss, recv_sem=rs,
            device_id={"group": group, "tensor": tensor}, device_id_type=MESH,
        )

    barrier = pltpu.get_barrier_semaphore()

    def xy_peer(k):
        return (yh if k < 4 else 1 - yh), lax.rem(x + k % 4, 4)

    for k in range(1, 8):
        pl.semaphore_signal(barrier, inc=1, device_id={"group": group_of(yh, lax.rem(z + k, 8), x), "tensor": t}, device_id_type=MESH)
    for k in range(1, 8):
        yh_, x_ = xy_peer(k)
        pl.semaphore_signal(barrier, inc=1, device_id={"group": group_of(yh_, z, x_), "tensor": t}, device_id_type=MESH)
    for k in range(1, 4):
        pl.semaphore_signal(barrier, inc=1, device_id={"group": g, "tensor": tensor_of(k)}, device_id_type=MESH)

    def arrived(ref, sem):
        remote(ref, ref, ts, sem, g, t).wait_recv()

    def left(ref, sem):
        remote(ref, ref, sem, tr, g, t).wait_send()

    def load(src, dst, i):
        copy = pltpu.make_async_copy(src, dst, lsem.at[i])
        copy.start()
        return copy

    l_dk = load(dkv_hbm.at[pl.ds(pl.multiple_of(t * 16, 16), 16), :], dk_v, 0)
    l_uk = load(ukv_hbm, uk_v, 1)
    l_do = load(do_hbm, do_v, 2)
    l_uo = load(uo_hbm, uo_v, 3)
    l_hid = load(hid_hbm, hid, 4)
    l_q = load(q_hbm, q_v, 5)
    l_fkv = load(fkv_hbm, fkv, 6)
    l_kv = load(kv_hbm, kv, 7)
    l_len = load(len_hbm, len_ref, 9)
    l_w = load(w_hbm, w, 8)

    s4[...] = jnp.zeros_like(s4)
    l_dk.wait()
    l_uk.wait()
    l_do.wait()
    for h in range(8):
        s16[2 * h : 2 * h + 2, :] = do_v[h].astype(F32)
    for k in range(2):
        s4[2 * k : 2 * k + 2, :] = uk_v[k].astype(F32)
    package = (
        dot(dk_v[...], place(64, 128, 0))
        + dot(s16[...].astype(BF), place(32, 128, 64))
        + dot(s4[...].astype(BF), place(32, 128, 96))
    )
    ga[yh, z, x] = package.astype(BF)
    l_uo.wait()

    @pl.when(yh == c)
    def _():
        up = uo_v[...]
        gb[z, x] = (dot(up[0:16], place(64, 128, 0)) + dot(up[16:32], place(64, 128, 64))).astype(BF)

    pl.semaphore_wait(barrier, 17)

    for k in (4, 3, 5, 2, 6, 1, 7):
        remote(ga.at[yh, z, x], ga.at[yh, z, x], a1s, a1r, group_of(yh, lax.rem(z + k, 8), x), t).start()

    @pl.when(yh == c)
    def _():
        for k in (4, 3, 5, 2, 6, 1, 7):
            remote(gb.at[z, x], gb.at[z, x], b1s, b1r, group_of(yh, lax.rem(z + k, 8), x), t).start()

    l_hid.wait()
    row = lax.broadcasted_iota(jnp.int32, (128, 512), 0)
    col = lax.broadcasted_iota(jnp.int32, (128, 512), 1)
    spread = jnp.where(jnp.where(col < 256, col, col - 257) == 2 * row, 1.0, 0.0).astype(BF)

    def spread_chunk(a, _):
        part = dot(hid[:, pl.ds(pl.multiple_of(a * 128, 128), 128)], spread).astype(BF)
        at = pl.ds(pl.multiple_of(a * 256, 256), 256)
        hx[0:32, at] = part[:, :256]
        hx[32:64, at] = part[:, 256:]
        return 0

    lax.fori_loop(0, 32, spread_chunk, 0, unroll=8)

    arrived(ga.at[yh, 0:7, x], a1r)
    for k in (6, 2, 5, 7, 4, 1, 3):
        yh_, x_ = xy_peer(k)
        remote(ga.at[yh, :, x], ga.at[yh, :, x], a2s, a2r, group_of(yh_, z, x_), t).start()

    @pl.when(yh == c)
    def _():
        arrived(gb.at[0:7, x], b1r)
        for k in (6, 2, 5, 7, 4, 1, 3):
            yh_, x_ = xy_peer(k)
            remote(gb.at[:, x], gb.at[:, x], b2s, b2r, group_of(yh_, z, x_), t).start()

    l_fkv.wait()

    def project(a, total):
        at = pl.ds(pl.multiple_of(a * 1024, 1024), 1024)
        return total + dot(hx[:, at], fkv[at, :])

    base[...] = lax.fori_loop(0, 8, project, jnp.zeros((64, 128), F32), unroll=4)

    l_len.wait()
    sub = lax.broadcasted_iota(jnp.int32, (32, 128), 0)
    lane = lax.broadcasted_iota(jnp.int32, (32, 128), 1)
    later = jnp.where(sub >= 16, 1, 0)
    in_step = sub - 16 * later
    position = later
    for r in range(16):
        position = position + jnp.where(in_step == r, len_ref[r], 0)
    counter = jnp.where(lane < 64, lane, lane - 64).astype(F32)
    angle = position.astype(F32) * jnp.exp(counter * (-2.0 * math.log(ROPE_BASE) / 128))
    cosine = jnp.cos(angle)
    sine = jnp.sin(angle)
    sine = jnp.where(lane < 64, -sine, sine)

    l_q.wait()
    for s in range(2):
        qs[:, s * 8 : s * 8 + 8, :] = q_v[s].astype(F32)
    l_kv.wait()
    slots = lax.broadcasted_iota(jnp.int32, (16, 256), 1)

    def cached(r, _):
        scores = dot_nt(qs[r].astype(BF), kv[r]) * SCALE
        scores = jnp.where(slots < len_ref[r], scores, MASKED)
        top = jnp.max(scores, axis=1, keepdims=True)
        expo = jnp.exp(scores - top)
        acc[r] = dot(expo.astype(BF), kv[16 + r])
        mm[r] = jnp.broadcast_to(top, (16, 128))
        ll[r] = jnp.broadcast_to(jnp.sum(expo, axis=1, keepdims=True), (16, 128))
        return 0

    lax.fori_loop(0, 16, cached, 0, unroll=8)
    u[...] = jnp.zeros_like(u)

    arrived(ga.at[:, 0:7], a2r)
    for y_ in range(2):
        for z_ in range(8):
            first = (y_ * 8 + z_) * 64
            gf[first : first + 64, :] = ga[y_, z_].astype(F32).reshape(64, 128)
    lane16 = lax.broadcasted_iota(jnp.int32, (16, 128), 1)

    def down_chunk(a, _):
        even = gf[pl.ds(pl.multiple_of(a * 32, 32), 16), :]
        odd = gf[pl.ds(pl.multiple_of(a * 32 + 16, 16), 16), :]
        gt[:, pl.ds(pl.multiple_of(a * 128, 128), 128)] = jnp.where(lane16 < 64, even, pltpu.roll(odd, 64, 1)).astype(BF)
        return 0

    lax.fori_loop(0, 32, down_chunk, 0, unroll=8)
    low = dot_nt(hid[...], gt[...]).astype(BF)
    zs[...] = dot(low, place(16, 128, 96 + 16 * c)).astype(BF)
    for k in (2, 3, 1):
        remote(zs, zr.at[k], ts, tr, g, tensor_of(k)).start()

    for j in range(16):
        dmf[pl.ds((j // 2) * 128 + j % 2, 64, stride=2), :] = gf[pl.ds(j, 64, stride=16), :]

    arrived(zr.at[1:4], tr)
    mine = (zs[...].astype(F32) + zr[1].astype(F32)).astype(BF)
    theirs = (zr[2].astype(F32) + zr[3].astype(F32)).astype(BF)
    is_key = (yl == 0).astype(F32)
    z_key = (mine.astype(F32) * is_key + theirs.astype(F32) * (1.0 - is_key)).astype(BF)
    z_value = (mine.astype(F32) * (1.0 - is_key) + theirs.astype(F32) * is_key).astype(BF)
    key = base[0:32, :] + ADAPTER_SCALE * dot_nt(z_key, dmf[0:128, :].astype(BF))
    value = base[32:64, :] + ADAPTER_SCALE * dot_nt(z_value, dmf[128:256, :].astype(BF))
    key = (key * cosine + pltpu.roll(key, 64, 1) * sine).astype(BF)
    value = value.astype(BF)
    nk[...] = key.astype(F32)
    nv[...] = value.astype(F32)
    for s in range(2):
        nst[s, 0] = key[s * 16 : s * 16 + 16]
        nst[s, 1] = value[s * 16 : s * 16 + 16]
    l_nkv = pltpu.make_async_copy(nst, nkv_hbm, outk)
    l_nkv.start()

    first_step = lax.broadcasted_iota(jnp.int32, (16, 128), 0) < 8
    for r in range(16):
        query = qs[r]
        s0 = jnp.sum(query * nk[r : r + 1, :], axis=1, keepdims=True) * SCALE
        s1 = jnp.sum(query * nk[16 + r : 17 + r, :], axis=1, keepdims=True) * SCALE
        s0 = jnp.broadcast_to(s0, (16, 128))
        s1 = jnp.where(first_step, MASKED, jnp.broadcast_to(s1, (16, 128)))
        top = jnp.maximum(mm[r], jnp.maximum(s0, s1))
        alpha = jnp.exp(mm[r] - top)
        p0 = jnp.exp(s0 - top)
        p1 = jnp.exp(s1 - top)
        total = alpha * ll[r] + p0 + p1
        ctxs[r * 16 : r * 16 + 16, :] = (alpha * acc[r] + p0 * nv[r : r + 1, :] + p1 * nv[16 + r : 17 + r, :]) / total
    for s in range(2):
        for h in range(8):
            ctx[s * 16 : s * 16 + 16, h * 128 : h * 128 + 128] = ctxs[pl.ds(s * 8 + h, 16, stride=16), :].astype(BF)

    context = ctx[...]
    zos[...] = dot(context, dmf[...].astype(BF))
    for k in (2, 3, 1):
        remote(zos, zor.at[k], os, orr, g, tensor_of(k)).start()

    l_w.wait()
    core_peer = tensor_of(1)
    chip_peer = tensor_of(2)

    def columns(half, j):
        return pl.ds(pl.multiple_of(half * 2048 + j * 512, 512), 512)

    def give_copy(j):
        return remote(ps.at[j], pr.at[j], pss, prs.at[j], g, core_peer)

    def chip_copy(j):
        return remote(ys.at[j], yr.at[j], yss, yrs.at[j], g, chip_peer)

    def final_copy(j):
        return remote(fs.at[j], att_hbm.at[:, columns(c, j)], fss, frs, g, core_peer)

    def local_copy(j):
        return pltpu.make_async_copy(fs.at[j], att_hbm.at[:, columns(c, j)], outs)

    def give(j):
        ps[j] = dot(context, w[:, columns(1 - c, j)]).astype(BF)
        give_copy(j).start()

    def keep(j):
        part = dot(context, w[:, columns(c, j)])
        give_copy(j).wait_recv()
        ys[j] = (part + pr[j].astype(F32)).astype(BF)
        chip_copy(j).start()

    def finish(j):
        term = dot(low_sum, u[:, j * 512 : j * 512 + 512])
        chip_copy(j).wait_recv()
        fs[j] = ((ys[j].astype(F32) + yr[j].astype(F32)) + term).astype(BF)
        final_copy(j).start()
        local_copy(j).start()

    give(0)
    give(1)
    keep(0)
    give(2)
    keep(1)
    give(3)
    keep(2)
    keep(3)

    @pl.when(yh == c)
    def _():
        arrived(gb.at[:, 0:3], b2r)

    @pl.when(yh != c)
    def _():
        arrived(gb, b2r)

    for a in range(16):
        even = gb[a // 2, 2 * (a % 2)].astype(F32)
        odd = gb[a // 2, 2 * (a % 2) + 1].astype(F32)
        u[64:80, a * 128 : a * 128 + 128] = jnp.where(lane16 < 64, even, pltpu.roll(odd, 64, 1)).astype(BF)
        u[80:96, a * 128 : a * 128 + 128] = jnp.where(lane16 < 64, pltpu.roll(even, 64, 1), odd).astype(BF)
    arrived(zor.at[1:4], orr)
    low_sum = (zos[...] + zor[1]) + (zor[2] + zor[3])
    low_sum = jnp.where(jnp.logical_and(lane >= 64, lane < 96), ADAPTER_SCALE * low_sum, 0.0).astype(BF)
    for j in range(4):
        finish(j)

    left(ga.at[yh, 0:7, x], a1s)
    left(ga.at[:, 0:7], a2s)
    left(zr.at[1:4], ts)
    left(zor.at[1:4], os)
    left(ps, pss)
    left(ys, yss)
    left(fs, fss)

    @pl.when(yh == c)
    def _():
        left(ga.at[yh, 0:7, x], b1s)
        left(ga.at[:, 0:7], b2s)

    l_nkv.wait()
    pltpu.make_async_copy(fs, fs, outs).wait()
    arrived(fs, frs)


def local(hidden, queries, kv_cache, lengths, frozen_key_value, frozen_output_weight, down_kv, up_kv, down_o, up_o):
    hbm = pl.BlockSpec(memory_space=pltpu.HBM)
    dma = pltpu.SemaphoreType.DMA
    args = (
        hidden.reshape(32, 4096),
        queries,
        kv_cache.reshape(32, 256, 128),
        lengths,
        frozen_key_value.reshape(8192, 128),
        frozen_output_weight,
        down_kv.transpose(1, 2, 0).reshape(64, 64),
        up_kv.transpose(0, 2, 3, 1).reshape(2, 2, 32),
        down_o,
        up_o,
    )
    args = tuple(pltpu.with_memory_space_constraint(a, pltpu.HBM) for a in args)
    v = pltpu.VMEM
    attended, new_kv = pl.pallas_call(
        kernel,
        out_shape=(pltpu.VMEM((32, 4096), BF), pltpu.VMEM((2, 2, 16, 128), BF)),
        in_specs=[hbm] * 10,
        out_specs=(hbm, hbm),
        scratch_shapes=[
            v((32, 4096), BF), v((2, 16, 8, 128), BF), v((32, 256, 128), BF), v((8192, 128), BF), v((1024, 4096), BF),
            v((16, 64), BF), v((2, 2, 32), BF), v((8, 2, 32), BF), v((32, 64), BF),
            v((64, 8192), BF), v((16, 16, 128), F32), v((2, 8, 4, 16, 128), BF), v((8, 4, 16, 128), BF),
            v((16, 4096), BF), v((1024, 128), F32), v((1024, 128), F32), v((16, 32), F32), v((16, 32), F32),
            v((32, 128), BF), v((4, 32, 128), BF), v((32, 128), F32), v((4, 32, 128), F32),
            v((16, 16, 128), F32), v((16, 16, 128), F32), v((16, 16, 128), F32), v((256, 128), F32),
            v((32, 1024), BF), v((128, 2048), BF),
            v((4, 32, 512), BF), v((4, 32, 512), BF), v((4, 32, 512), BF), v((4, 32, 512), BF), v((4, 32, 512), BF),
            v((32, 128), F32), v((32, 128), F32), v((2, 2, 16, 128), BF), v((64, 128), F32), pltpu.SMEM((16,), jnp.int32),
            dma((10,)), dma((18,)), dma((4,)), dma((4,)),
        ],
        compiler_params=pltpu.CompilerParams(
            collective_id=0, has_side_effects=True, vmem_limit_bytes=40 * 1024 * 1024
        ),
    )(*args)
    return attended.reshape(2, 16, 4096), new_kv.reshape(2, 2, 16, 1, 128)


def solution(mesh):
    placed = (
        P(None, "group", None),
        P(None, "group", "tensor", None),
        P(None, "group", "tensor", None, None),
        P("group"),
        P(None, None, "tensor"),
        P("tensor", None),
        P("group", None, None),
        P(None, None, "tensor", "group"),
        P("tensor", "group", None),
        P(None, "group"),
    )
    return jax.shard_map(
        local,
        mesh=mesh,
        in_specs=placed,
        out_specs=(P(None, "group", None), P(None, None, "group", "tensor", None)),
        check_vma=False,
    )
```

```python
import math

import jax
import jax.numpy as jnp
from jax import lax
from jax.experimental import pallas as pl
from jax.experimental.pallas import tpu as pltpu
from jax.sharding import PartitionSpec as P

BF = jnp.bfloat16
F32 = jnp.float32
MESH = pl.DeviceIdType.MESH

ADAPTER_SCALE = 2.0
ROPE_BASE = 500000.0
SCALE = 1.0 / math.sqrt(128.0)
MASKED = -1e30

NT = (((1,), (1,)), ((), ()))


def dot(a, b):
    return jnp.dot(a, b, preferred_element_type=F32)


def dot_nt(a, b):
    return lax.dot_general(a, b, NT, preferred_element_type=F32)


def place(rows, columns, offset):
    i = lax.broadcasted_iota(jnp.int32, (rows, columns), 0)
    j = lax.broadcasted_iota(jnp.int32, (rows, columns), 1)
    return jnp.where(j == i + offset, 1.0, 0.0).astype(BF)


def kernel(
    hid_hbm, q_hbm, kv_hbm, len_hbm, fkv_hbm, w_hbm, dkv_hbm, ukv_hbm, do_hbm, uo_hbm,
    att_hbm, nkv_hbm,
    hid, q_v, kv, fkv, w, dk_v, uk_v, do_v, uo_v,
    hx, qs, r1, gb, gt, uo, hd, pm, dm, s16, s4,
    zs, zr, zos, zor, acc, mm, ll, ctxs, ctx, u,
    ps, pr, ys, yr, fs, nk, nv, nst, base, len_ref,
    lsem, one, prs, yrs,
):
    a1s, a1r, a2s, a2r, b1s, b1r, b2s, b2r, ts, tr, os, orr, pss, yss, fss, frs, outs, outk, c2s, c2r = (one.at[i] for i in range(20))
    g = lax.axis_index("group")
    t = lax.axis_index("tensor")
    yh = lax.div(g, 32)
    z = lax.rem(lax.div(g, 4), 8)
    x = lax.rem(g, 4)
    yl = lax.div(t, 2)
    c = lax.rem(t, 2)

    def group_of(yh_, z_, x_):
        return yh_ * 32 + z_ * 4 + x_

    def tensor_of(k):
        yl_ = yl if k < 2 else 1 - yl
        c_ = c if k % 2 == 0 else 1 - c
        return yl_ * 2 + c_

    def remote(src, dst, ss, rs, group, tensor):
        return pltpu.make_async_remote_copy(
            src_ref=src, dst_ref=dst, send_sem=ss, recv_sem=rs,
            device_id={"group": group, "tensor": tensor}, device_id_type=MESH,
        )

    def arrived(ref, sem):
        remote(ref, ref, ts, sem, g, t).wait_recv()

    def left(ref, sem):
        remote(ref, ref, sem, tr, g, t).wait_send()

    def load(src, dst, i):
        copy = pltpu.make_async_copy(src, dst, lsem.at[i])
        copy.start()
        return copy

    l_dk = load(dkv_hbm.at[pl.ds(pl.multiple_of(c * 32, 32), 32), :], dk_v, 0)
    l_uk = load(ukv_hbm, uk_v, 1)
    l_do = load(do_hbm, do_v, 2)
    l_uo = load(uo_hbm, uo_v, 3)

    barrier = pltpu.get_barrier_semaphore()

    def xy_peer(k):
        return (yh if k < 4 else 1 - yh), lax.rem(x + k % 4, 4)

    for k in range(1, 8):
        pl.semaphore_signal(barrier, inc=1, device_id={"group": group_of(yh, lax.rem(z + k, 8), x), "tensor": t}, device_id_type=MESH)
    for k in range(1, 8):
        yh_, x_ = xy_peer(k)
        pl.semaphore_signal(barrier, inc=1, device_id={"group": group_of(yh_, z, x_), "tensor": t}, device_id_type=MESH)
    for k in range(1, 4):
        pl.semaphore_signal(barrier, inc=1, device_id={"group": g, "tensor": tensor_of(k)}, device_id_type=MESH)

    l_hid = load(hid_hbm, hid, 4)
    l_q = load(q_hbm, q_v, 5)
    l_fkv = load(fkv_hbm, fkv, 6)
    l_kv = load(kv_hbm, kv, 7)
    l_len = load(len_hbm, len_ref, 9)
    l_w = load(w_hbm, w, 8)

    m = lax.rem(z, 4)
    q = lax.rem(m + jnp.where(z < 4, 1, 2), 4)
    l_dk.wait()
    l_uk.wait()
    l_do.wait()
    for h in range(8):
        s16[2 * h : 2 * h + 2, :] = do_v[h].astype(F32)
    for k in range(2):
        for i in range(4):
            s4[4 * i + 2 * k : 4 * i + 2 * k + 2, :] = uk_v[k].astype(F32)
    row16 = lax.broadcasted_iota(jnp.int32, (16, 32), 0)
    up_rows = jnp.where(jnp.logical_and(row16 >= 4 * m, row16 < 4 * m + 4), s4[...], 0.0)
    half = dk_v[...]
    r1[z, 0] = (dot(half[0:16], place(64, 128, 0)) + dot(half[16:32], place(64, 128, 64))).astype(BF)
    r1[z, 1] = (
        dot(s16[...].astype(BF), place(32, 128, 32 * m)) + dot(up_rows.astype(BF), place(32, 128, 32 * q))
    ).astype(BF)
    l_uo.wait()

    @pl.when(yh == c)
    def _():
        up = uo_v[...]
        gb[z, x] = (dot(up[0:16], place(64, 128, 0)) + dot(up[16:32], place(64, 128, 64))).astype(BF)

    pl.semaphore_wait(barrier, 17)

    for k in (4, 3, 5, 2, 6, 1, 7):
        remote(r1.at[z], r1.at[z], a1s, a1r, group_of(yh, lax.rem(z + k, 8), x), t).start()

    @pl.when(yh == c)
    def _():
        for k in (4, 3, 5, 2, 6, 1, 7):
            remote(gb.at[z, x], gb.at[z, x], b1s, b1r, group_of(yh, lax.rem(z + k, 8), x), t).start()

    l_hid.wait()
    row = lax.broadcasted_iota(jnp.int32, (128, 512), 0)
    col = lax.broadcasted_iota(jnp.int32, (128, 512), 1)
    spread = jnp.where(jnp.where(col < 256, col, col - 257) == 2 * row, 1.0, 0.0).astype(BF)

    def spread_chunk(a, _):
        part = dot(hid[:, pl.ds(pl.multiple_of(a * 128, 128), 128)], spread).astype(BF)
        at = pl.ds(pl.multiple_of(a * 256, 256), 256)
        hx[0:32, at] = part[:, :256]
        hx[32:64, at] = part[:, 256:]
        return 0

    lax.fori_loop(0, 32, spread_chunk, 0, unroll=8)

    lane16 = lax.broadcasted_iota(jnp.int32, (16, 128), 1)
    block = yh * 4 + x
    arrived(r1.at[0:7], a1r)
    for z_ in range(8):
        gt[:, pl.ds(pl.multiple_of(block * 1024 + z_ * 128, 128), 128)] = r1[z_, 0]
    own_lanes = gt.at[:, pl.ds(pl.multiple_of(block * 1024, 1024), 1024)]
    for k in (6, 2, 5, 7, 4, 1, 3):
        yh_, x_ = xy_peer(k)
        remote(own_lanes, own_lanes, a2s, a2r, group_of(yh_, z, x_), t).start()
    others = [r1[z_, 1].astype(F32) for z_ in range(8)]

    def lanes_of(z_, i):
        return jnp.where(jnp.logical_and(lane16 >= 32 * i, lane16 < 32 * i + 32), others[z_], 0.0)

    uo[block, 0:16] = sum(lanes_of(z_, (z_ % 4 + 1 + z_ // 4) % 4) for z_ in range(8)).astype(BF)
    uo[block, 16:32] = sum(lanes_of(z_, z_) for z_ in range(4)).astype(BF)
    uo[block, 32:48] = sum(lanes_of(z_, z_ - 4) for z_ in range(4, 8)).astype(BF)
    for k in (6, 2, 5, 7, 4, 1, 3):
        yh_, x_ = xy_peer(k)
        remote(uo.at[block], uo.at[block], c2s, c2r, group_of(yh_, z, x_), t).start()

    @pl.when(yh == c)
    def _():
        arrived(gb.at[0:7, x], b1r)
        for k in (6, 2, 5, 7, 4, 1, 3):
            yh_, x_ = xy_peer(k)
            remote(gb.at[:, x], gb.at[:, x], b2s, b2r, group_of(yh_, z, x_), t).start()

    lane = lax.broadcasted_iota(jnp.int32, (32, 128), 1)
    for a in range(32):
        pair = hid[:, a * 128 : a * 128 + 128].astype(F32)
        turned = pltpu.roll(pair, 64, 1)
        at = ((a // 16) * 4 + 2 * (a % 2)) * 1024 + (a // 2 % 8) * 128
        hd[0:32, at : at + 128] = jnp.where(lane < 64, pair, 0.0).astype(BF)
        hd[32:64, at : at + 128] = jnp.where(lane < 64, 0.0, turned).astype(BF)
        at = at + 1024
        hd[0:32, at : at + 128] = jnp.where(lane < 64, turned, 0.0).astype(BF)
        hd[32:64, at : at + 128] = jnp.where(lane < 64, 0.0, pair).astype(BF)

    feature = lax.broadcasted_iota(jnp.int32, (128, 384), 0)
    source = lax.broadcasted_iota(jnp.int32, (128, 384), 1)

    def digit(value, shift, mask):
        return jnp.bitwise_and(lax.shift_right_logical(value, shift), mask)

    first = (digit(feature, 6, 1) * 4 + digit(feature, 1, 3)) * 48 + digit(feature, 0, 1)
    from_up = first + 4 * digit(feature, 3, 3)
    from_down = first + 16 + 16 * digit(feature, 5, 1)
    for i in range(2):
        pm[i] = jnp.where(source == from_up + 2 * i, 1.0, 0.0).astype(BF)
    for h in range(8):
        pm[2 + h] = jnp.where(source == from_down + 2 * h, 1.0, 0.0).astype(BF)
    square = lax.broadcasted_iota(jnp.int32, (128, 128), 0)
    lane_group = digit(lax.broadcasted_iota(jnp.int32, (128, 128), 1), 5, 3)
    up_lanes = lane_group == digit(digit(square, 3, 3) + 1 + digit(square, 5, 1), 0, 3)
    down_lanes = lane_group == digit(square, 3, 3)

    l_fkv.wait()

    def project(a, total):
        at = pl.ds(pl.multiple_of(a * 1024, 1024), 1024)
        return total + dot(hx[:, at], fkv[at, :])

    base[...] = lax.fori_loop(0, 8, project, jnp.zeros((64, 128), F32), unroll=4)

    l_len.wait()
    sub = lax.broadcasted_iota(jnp.int32, (32, 128), 0)
    later = jnp.where(sub >= 16, 1, 0)
    in_step = sub - 16 * later
    position = later
    for r in range(16):
        position = position + jnp.where(in_step == r, len_ref[r], 0)
    counter = jnp.where(lane < 64, lane, lane - 64).astype(F32)
    angle = position.astype(F32) * jnp.exp(counter * (-2.0 * math.log(ROPE_BASE) / 128))
    cosine = jnp.cos(angle)
    sine = jnp.sin(angle)
    sine = jnp.where(lane < 64, -sine, sine)

    l_q.wait()
    for s in range(2):
        qs[:, s * 8 : s * 8 + 8, :] = q_v[s].astype(F32)
    l_kv.wait()
    slots = lax.broadcasted_iota(jnp.int32, (16, 256), 1)

    def cached(r, _):
        scores = dot_nt(qs[r].astype(BF), kv[r]) * SCALE
        scores = jnp.where(slots < len_ref[r], scores, MASKED)
        top = jnp.max(scores, axis=1, keepdims=True)
        expo = jnp.exp(scores - top)
        acc[r] = dot(expo.astype(BF), kv[16 + r])
        mm[r] = jnp.broadcast_to(top, (16, 128))
        ll[r] = jnp.broadcast_to(jnp.sum(expo, axis=1, keepdims=True), (16, 128))
        return 0

    lax.fori_loop(0, 16, cached, 0, unroll=8)
    u[...] = jnp.zeros_like(u)

    rank = lax.broadcasted_iota(jnp.int32, (16, 128), 0)
    arrived(gt.at[:, 0:7168], a2r)
    low = dot_nt(hd[...], gt[...]).astype(BF)
    repeat = [jnp.where(digit(lane16, 0, 31) == rank + 16 * i, 1.0, 0.0).astype(BF) for i in range(2)]
    zs[...] = (dot(low[0:32], repeat[0]) + dot(low[32:64], repeat[1])).astype(BF)
    remote(zs, zr, ts, tr, g, tensor_of(1)).start()

    arrived(uo.at[0:7], c2r)
    gathered = uo[...].reshape(384, 128)
    up_key = jnp.where(up_lanes, dot(pm[0], gathered), 0.0).astype(BF)
    up_value = jnp.where(up_lanes, dot(pm[1], gathered), 0.0).astype(BF)
    for h in range(8):
        dm[h * 128 : h * 128 + 128, :] = jnp.where(down_lanes, dot(pm[2 + h], gathered), 0.0).astype(BF)

    arrived(zr, tr)
    z_key = jnp.where(c == 0, zs[...], zr[...])
    z_value = jnp.where(c == 0, zr[...], zs[...])
    key = base[0:32, :] + ADAPTER_SCALE * dot_nt(z_key, up_key)
    value = base[32:64, :] + ADAPTER_SCALE * dot_nt(z_value, up_value)
    key = (key * cosine + pltpu.roll(key, 64, 1) * sine).astype(BF)
    value = value.astype(BF)
    nk[...] = key.astype(F32)
    nv[...] = value.astype(F32)
    for s in range(2):
        nst[s, 0] = key[s * 16 : s * 16 + 16]
        nst[s, 1] = value[s * 16 : s * 16 + 16]
    l_nkv = pltpu.make_async_copy(nst, nkv_hbm, outk)
    l_nkv.start()

    first_step = lax.broadcasted_iota(jnp.int32, (16, 128), 0) < 8
    for r in range(16):
        query = qs[r]
        s0 = jnp.sum(query * nk[r : r + 1, :], axis=1, keepdims=True) * SCALE
        s1 = jnp.sum(query * nk[16 + r : 17 + r, :], axis=1, keepdims=True) * SCALE
        s0 = jnp.broadcast_to(s0, (16, 128))
        s1 = jnp.where(first_step, MASKED, jnp.broadcast_to(s1, (16, 128)))
        top = jnp.maximum(mm[r], jnp.maximum(s0, s1))
        alpha = jnp.exp(mm[r] - top)
        p0 = jnp.exp(s0 - top)
        p1 = jnp.exp(s1 - top)
        total = alpha * ll[r] + p0 + p1
        ctxs[r * 16 : r * 16 + 16, :] = (alpha * acc[r] + p0 * nv[r : r + 1, :] + p1 * nv[16 + r : 17 + r, :]) / total
    for s in range(2):
        for h in range(8):
            ctx[s * 16 : s * 16 + 16, h * 128 : h * 128 + 128] = ctxs[pl.ds(s * 8 + h, 16, stride=16), :].astype(BF)

    context = ctx[...]
    zos[...] = dot(context, dm[...])
    for k in (2, 3, 1):
        remote(zos, zor.at[k], os, orr, g, tensor_of(k)).start()

    l_w.wait()
    core_peer = tensor_of(1)
    chip_peer = tensor_of(2)

    def columns(half, j):
        return pl.ds(pl.multiple_of(half * 2048 + j * 512, 512), 512)

    def give_copy(j):
        return remote(ps.at[j], pr.at[j], pss, prs.at[j], g, core_peer)

    def chip_copy(j):
        return remote(ys.at[j], yr.at[j], yss, yrs.at[j], g, chip_peer)

    def final_copy(j):
        return remote(fs.at[j], att_hbm.at[:, columns(c, j)], fss, frs, g, core_peer)

    def local_copy(j):
        return pltpu.make_async_copy(fs.at[j], att_hbm.at[:, columns(c, j)], outs)

    def give(j):
        ps[j] = dot(context, w[:, columns(1 - c, j)]).astype(BF)
        give_copy(j).start()

    def keep(j):
        part = dot(context, w[:, columns(c, j)])
        give_copy(j).wait_recv()
        ys[j] = (part + pr[j].astype(F32)).astype(BF)
        chip_copy(j).start()

    def finish(j):
        term = dot(low_sum, u[:, j * 512 : j * 512 + 512])
        chip_copy(j).wait_recv()
        fs[j] = ((ys[j].astype(F32) + yr[j].astype(F32)) + term).astype(BF)
        final_copy(j).start()
        local_copy(j).start()

    for j in range(4):
        give(j)
    for j in range(4):
        keep(j)

    @pl.when(yh == c)
    def _():
        arrived(gb.at[:, 0:3], b2r)

    @pl.when(yh != c)
    def _():
        arrived(gb, b2r)

    for a in range(16):
        even = gb[a // 2, 2 * (a % 2)].astype(F32)
        odd = gb[a // 2, 2 * (a % 2) + 1].astype(F32)
        u[64:80, a * 128 : a * 128 + 128] = jnp.where(lane16 < 64, even, pltpu.roll(odd, 64, 1)).astype(BF)
        u[80:96, a * 128 : a * 128 + 128] = jnp.where(lane16 < 64, pltpu.roll(even, 64, 1), odd).astype(BF)
    arrived(zor.at[1:4], orr)
    low_sum = (zos[...] + zor[1]) + (zor[2] + zor[3])
    low_sum = low_sum + pltpu.roll(low_sum, 64, 1)
    low_sum = low_sum + pltpu.roll(low_sum, 32, 1)
    low_sum = jnp.where(jnp.logical_and(lane >= 64, lane < 96), ADAPTER_SCALE * low_sum, 0.0).astype(BF)
    for j in range(4):
        finish(j)

    left(r1.at[0:7], a1s)
    left(gt.at[:, 0:7168], a2s)
    left(uo.at[0:7], c2s)
    left(zs, ts)
    left(zor.at[1:4], os)
    left(ps, pss)
    left(ys, yss)
    left(fs, fss)

    @pl.when(yh == c)
    def _():
        left(gb.at[0:7, x], b1s)
        left(gt.at[:, 0:7168], b2s)

    l_nkv.wait()
    pltpu.make_async_copy(fs, fs, outs).wait()
    arrived(fs, frs)


def store(att_in, nkv_in, att_out, nkv_out, sems):
    first = pltpu.make_async_copy(att_in, att_out, sems.at[0])
    second = pltpu.make_async_copy(nkv_in, nkv_out, sems.at[1])
    first.start()
    second.start()
    first.wait()
    second.wait()


def local(hidden, queries, kv_cache, lengths, frozen_key_value, frozen_output_weight, down_kv, up_kv, down_o, up_o):
    hbm = pl.BlockSpec(memory_space=pltpu.HBM)
    dma = pltpu.SemaphoreType.DMA
    args = (
        hidden.reshape(32, 4096),
        queries,
        kv_cache.reshape(32, 256, 128),
        lengths,
        frozen_key_value.reshape(8192, 128),
        frozen_output_weight,
        down_kv.transpose(1, 2, 0).reshape(64, 64),
        up_kv.transpose(0, 2, 3, 1).reshape(2, 2, 32),
        down_o,
        up_o,
    )
    args = tuple(pltpu.with_memory_space_constraint(a, pltpu.HBM) for a in args)
    v = pltpu.VMEM
    attended, new_kv = pl.pallas_call(
        kernel,
        out_shape=(pltpu.VMEM((32, 4096), BF), pltpu.VMEM((2, 2, 16, 128), BF)),
        in_specs=[hbm] * 10,
        out_specs=(hbm, hbm),
        scratch_shapes=[
            v((32, 4096), BF), v((2, 16, 8, 128), BF), v((32, 256, 128), BF), v((8192, 128), BF), v((1024, 4096), BF),
            v((32, 64), BF), v((2, 2, 32), BF), v((8, 2, 32), BF), v((32, 64), BF),
            v((64, 8192), BF), v((16, 16, 128), F32), v((8, 2, 16, 128), BF), v((8, 4, 16, 128), BF),
            v((16, 8192), BF), v((8, 48, 128), BF), v((64, 8192), BF), v((10, 128, 384), BF), v((1024, 128), BF),
            v((16, 32), F32), v((16, 32), F32),
            v((32, 128), BF), v((32, 128), BF), v((32, 128), F32), v((4, 32, 128), F32),
            v((16, 16, 128), F32), v((16, 16, 128), F32), v((16, 16, 128), F32), v((256, 128), F32),
            v((32, 1024), BF), v((128, 2048), BF),
            v((4, 32, 512), BF), v((4, 32, 512), BF), v((4, 32, 512), BF), v((4, 32, 512), BF), v((4, 32, 512), BF),
            v((32, 128), F32), v((32, 128), F32), v((2, 2, 16, 128), BF), v((64, 128), F32), pltpu.SMEM((16,), jnp.int32),
            dma((10,)), dma((20,)), dma((4,)), dma((4,)),
        ],
        compiler_params=pltpu.CompilerParams(
            collective_id=0, has_side_effects=True, vmem_limit_bytes=40 * 1024 * 1024
        ),
    )(*args)
    attended, new_kv = pl.pallas_call(
        store,
        out_shape=(pltpu.HBM((32, 4096), BF), pltpu.HBM((2, 2, 16, 128), BF)),
        in_specs=[hbm, hbm],
        out_specs=(hbm, hbm),
        scratch_shapes=[dma((2,))],
    )(pltpu.with_memory_space_constraint(attended, pltpu.VMEM), pltpu.with_memory_space_constraint(new_kv, pltpu.VMEM))
    return attended.reshape(2, 16, 4096), new_kv.reshape(2, 2, 16, 1, 128)


def solution(mesh):
    placed = (
        P(None, "group", None),
        P(None, "group", "tensor", None),
        P(None, "group", "tensor", None, None),
        P("group"),
        P(None, None, "tensor"),
        P("tensor", None),
        P("group", None, None),
        P(None, None, "tensor", "group"),
        P("tensor", "group", None),
        P(None, "group"),
    )
    return jax.shard_map(
        local,
        mesh=mesh,
        in_specs=placed,
        out_specs=(P(None, "group", None), P(None, None, "group", "tensor", None)),
        check_vma=False,
    )
```

```python
import math

import jax
import jax.numpy as jnp
from jax import lax
from jax.experimental import pallas as pl
from jax.experimental.pallas import tpu as pltpu
from jax.sharding import PartitionSpec as P

BF = jnp.bfloat16
F32 = jnp.float32
MESH = pl.DeviceIdType.MESH

ADAPTER_SCALE = 2.0
ROPE_BASE = 500000.0
SCALE = 1.0 / math.sqrt(128.0)
MASKED = -1e30
WIDTH = 512

NT = (((1,), (1,)), ((), ()))


def dot(a, b):
    return jnp.dot(a, b, preferred_element_type=F32)


def dot_nt(a, b):
    return lax.dot_general(a, b, NT, preferred_element_type=F32)


def place(rows, columns, offset):
    i = lax.broadcasted_iota(jnp.int32, (rows, columns), 0)
    j = lax.broadcasted_iota(jnp.int32, (rows, columns), 1)
    return jnp.where(j == i + offset, 1.0, 0.0).astype(BF)


def kernel(
    hid_hbm, q_hbm, kv_hbm, len_hbm, fkv_hbm, w_hbm, dkv_hbm, ukv_hbm, do_hbm, uo_hbm,
    att_hbm, nkv_hbm,
    hid, q_v, kv, fkv, w, dk_v, uk_v, do_v, uo_v,
    hx, qs, r1, gb, gt, uu, uo, hd, pu, pm, dm, s16, s4,
    zs, zr, zos, zor, acc, mm, ll, ctxs, ctx, u,
    ps, pr, ys, yr, fs, nk, nv, nst, base, len_ref,
    lsem, one, prs, yrs,
):
    a1s, a1r, a2s, a2r, b1s, b1r, b2s, b2r, ts, tr, os, orr, pss, yss, fss, frs, outs, outk, c2s, c2r, d2s, d2r = (one.at[i] for i in range(22))
    g = lax.axis_index("group")
    t = lax.axis_index("tensor")
    yh = lax.div(g, 32)
    z = lax.rem(lax.div(g, 4), 8)
    x = lax.rem(g, 4)
    yl = lax.div(t, 2)
    c = lax.rem(t, 2)

    def group_of(yh_, z_, x_):
        return yh_ * 32 + z_ * 4 + x_

    def tensor_of(k):
        yl_ = yl if k < 2 else 1 - yl
        c_ = c if k % 2 == 0 else 1 - c
        return yl_ * 2 + c_

    def remote(src, dst, ss, rs, group, tensor):
        return pltpu.make_async_remote_copy(
            src_ref=src, dst_ref=dst, send_sem=ss, recv_sem=rs,
            device_id={"group": group, "tensor": tensor}, device_id_type=MESH,
        )

    barrier = pltpu.get_barrier_semaphore()

    def xy_peer(k):
        return (yh if k < 4 else 1 - yh), lax.rem(x + k % 4, 4)

    def arrived(ref, sem):
        remote(ref, ref, ts, sem, g, t).wait_recv()

    def left(ref, sem):
        remote(ref, ref, sem, tr, g, t).wait_send()

    def load(src, dst, i):
        copy = pltpu.make_async_copy(src, dst, lsem.at[i])
        copy.start()
        return copy

    l_dk = load(dkv_hbm.at[pl.ds(pl.multiple_of(c * 32, 32), 32), :], dk_v, 0)
    l_uk = load(ukv_hbm, uk_v, 1)
    l_do = load(do_hbm, do_v, 2)
    l_uo = load(uo_hbm, uo_v, 3)

    def greet(group, tensor):
        pl.semaphore_signal(barrier, inc=1, device_id={"group": group, "tensor": tensor}, device_id_type=MESH)

    for hop, k in (
        ("xy", 6), ("z", 4), ("z", 3), ("z", 5), ("xy", 5), ("xy", 7), ("xy", 2), ("z", 2), ("z", 6),
        ("xy", 4), ("xy", 1), ("xy", 3), ("z", 1), ("z", 7), ("t", 2), ("t", 3), ("t", 1),
    ):
        if hop == "z":
            greet(group_of(yh, lax.rem(z + k, 8), x), t)
        elif hop == "xy":
            greet(group_of(xy_peer(k)[0], z, xy_peer(k)[1]), t)
        else:
            greet(g, tensor_of(k))

    l_hid = load(hid_hbm, hid, 4)
    l_q = load(q_hbm, q_v, 5)
    l_fkv = load(fkv_hbm, fkv, 6)
    l_kv = load(kv_hbm, kv, 7)
    l_len = load(len_hbm, len_ref, 9)
    l_w = load(w_hbm, w, 8)

    m = lax.rem(z, 4)
    q = lax.rem(m + jnp.where(z < 4, 1, 2), 4)
    l_dk.wait()
    l_uk.wait()
    l_do.wait()
    for h in range(8):
        s16[2 * h : 2 * h + 2, :] = do_v[h].astype(F32)
    for k in range(2):
        for i in range(4):
            s4[4 * i + 2 * k : 4 * i + 2 * k + 2, :] = uk_v[k].astype(F32)
    row16 = lax.broadcasted_iota(jnp.int32, (16, 32), 0)
    up_rows = jnp.where(jnp.logical_and(row16 >= 4 * m, row16 < 4 * m + 4), s4[...], 0.0)
    half = dk_v[...]
    r1[z, 0] = (dot(half[0:16], place(64, 128, 0)) + dot(half[16:32], place(64, 128, 64))).astype(BF)
    r1[z, 1] = (
        dot(s16[...].astype(BF), place(32, 128, 32 * m)) + dot(up_rows.astype(BF), place(32, 128, 32 * q))
    ).astype(BF)
    l_uo.wait()

    @pl.when(yh == c)
    def _():
        up = uo_v[...]
        gb[z, x] = (dot(up[0:16], place(64, 128, 0)) + dot(up[16:32], place(64, 128, 64))).astype(BF)

    lane = lax.broadcasted_iota(jnp.int32, (32, 128), 1)
    pl.semaphore_wait(barrier, 17)

    for k in (4, 3, 5, 2, 6, 1, 7):
        remote(r1.at[z], r1.at[z], a1s, a1r, group_of(yh, lax.rem(z + k, 8), x), t).start()

    feature = lax.broadcasted_iota(jnp.int32, (128, 256), 0)
    source = lax.broadcasted_iota(jnp.int32, (128, 256), 1)

    def digit(value, shift, mask):
        return jnp.bitwise_and(lax.shift_right_logical(value, shift), mask)

    tile = digit(feature, 6, 1) * 4 + digit(feature, 1, 3)
    from_up = (tile * 16 + 4 * digit(feature, 3, 3) + digit(feature, 0, 1))[:, :128]
    from_down = tile * 32 + 16 * digit(feature, 5, 1) + digit(feature, 0, 1)
    for i in range(2):
        pu[i] = jnp.where(source[:, :128] == from_up + 2 * i, 1.0, 0.0).astype(BF)
    for h in range(8):
        pm[h] = jnp.where(source == from_down + 2 * h, 1.0, 0.0).astype(BF)
    square = lax.broadcasted_iota(jnp.int32, (128, 128), 0)
    lane_group = digit(lax.broadcasted_iota(jnp.int32, (128, 128), 1), 5, 3)
    up_lanes = lane_group == digit(digit(square, 3, 3) + 1 + digit(square, 5, 1), 0, 3)
    down_lanes = lane_group == digit(square, 3, 3)

    l_len.wait()
    sub = lax.broadcasted_iota(jnp.int32, (32, 128), 0)
    later = jnp.where(sub >= 16, 1, 0)
    in_step = sub - 16 * later
    position = later
    for r in range(16):
        position = position + jnp.where(in_step == r, len_ref[r], 0)
    counter = jnp.where(lane < 64, lane, lane - 64).astype(F32)
    angle = position.astype(F32) * jnp.exp(counter * (-2.0 * math.log(ROPE_BASE) / 128))
    cosine = jnp.cos(angle)
    sine = jnp.sin(angle)
    sine = jnp.where(lane < 64, -sine, sine)

    l_hid.wait()
    row = lax.broadcasted_iota(jnp.int32, (128, 512), 0)
    col = lax.broadcasted_iota(jnp.int32, (128, 512), 1)
    spread = jnp.where(jnp.where(col < 256, col, col - 257) == 2 * row, 1.0, 0.0).astype(BF)

    def spread_chunk(a, _):
        part = dot(hid[:, pl.ds(pl.multiple_of(a * 128, 128), 128)], spread).astype(BF)
        at = pl.ds(pl.multiple_of(a * 256, 256), 256)
        hx[0:32, at] = part[:, :256]
        hx[32:64, at] = part[:, 256:]
        return 0

    lax.fori_loop(0, 32, spread_chunk, 0, unroll=8)

    for a in range(32):
        pair = hid[:, a * 128 : a * 128 + 128].astype(F32)
        turned = pltpu.roll(pair, 64, 1)
        at = ((a // 16) * 4 + 2 * (a % 2)) * 1024 + (a // 2 % 8) * 128
        hd[0:32, at : at + 128] = jnp.where(lane < 64, pair, 0.0).astype(BF)
        hd[32:64, at : at + 128] = jnp.where(lane < 64, 0.0, turned).astype(BF)
        at = at + 1024
        hd[0:32, at : at + 128] = jnp.where(lane < 64, turned, 0.0).astype(BF)
        hd[32:64, at : at + 128] = jnp.where(lane < 64, 0.0, pair).astype(BF)

    l_fkv.wait()

    def project(a, total):
        at = pl.ds(pl.multiple_of(a * 1024, 1024), 1024)
        return total + dot(hx[:, at], fkv[at, :])

    base[...] = lax.fori_loop(0, 8, project, jnp.zeros((64, 128), F32), unroll=4)

    lane16 = lax.broadcasted_iota(jnp.int32, (16, 128), 1)
    block = yh * 4 + x
    arrived(r1.at[0:7], a1r)
    for z_ in range(8):
        gt[:, pl.ds(pl.multiple_of(block * 1024 + z_ * 128, 128), 128)] = r1[z_, 0]
    own_lanes = gt.at[:, pl.ds(pl.multiple_of(block * 1024, 1024), 1024)]
    for k in (6, 2, 5, 7, 4, 1, 3):
        yh_, x_ = xy_peer(k)
        remote(own_lanes, own_lanes, a2s, a2r, group_of(yh_, z, x_), t).start()
    others = [r1[z_, 1].astype(F32) for z_ in range(8)]

    def lanes_of(z_, i):
        return jnp.where(jnp.logical_and(lane16 >= 32 * i, lane16 < 32 * i + 32), others[z_], 0.0)

    uu[block] = sum(lanes_of(z_, (z_ % 4 + 1 + z_ // 4) % 4) for z_ in range(8)).astype(BF)
    uo[block, 0:16] = sum(lanes_of(z_, z_) for z_ in range(4)).astype(BF)
    uo[block, 16:32] = sum(lanes_of(z_, z_ - 4) for z_ in range(4, 8)).astype(BF)
    for ref, sent, came in ((uu, c2s, c2r), (uo, d2s, d2r)):
        for k in (6, 2, 5, 7, 4, 1, 3):
            yh_, x_ = xy_peer(k)
            remote(ref.at[block], ref.at[block], sent, came, group_of(yh_, z, x_), t).start()

    @pl.when(yh == c)
    def _():
        for k in (4, 3, 5, 2, 6, 1, 7):
            remote(gb.at[z, x], gb.at[z, x], b1s, b1r, group_of(yh, lax.rem(z + k, 8), x), t).start()

    l_q.wait()
    for s in range(2):
        qs[:, s * 8 : s * 8 + 8, :] = q_v[s].astype(F32)
    l_kv.wait()
    slots = lax.broadcasted_iota(jnp.int32, (16, 256), 1)

    def cached(r, _):
        scores = dot_nt(qs[r].astype(BF), kv[r]) * SCALE
        scores = jnp.where(slots < len_ref[r], scores, MASKED)
        top = jnp.max(scores, axis=1, keepdims=True)
        expo = jnp.exp(scores - top)
        acc[r] = dot(expo.astype(BF), kv[16 + r])
        mm[r] = jnp.broadcast_to(top, (16, 128))
        ll[r] = jnp.broadcast_to(jnp.sum(expo, axis=1, keepdims=True), (16, 128))
        return 0

    lax.fori_loop(0, 16, cached, 0, unroll=8)
    u[...] = jnp.zeros_like(u)

    arrived(gt.at[:, 0:7168], a2r)
    zs[...] = dot_nt(hd[...], gt[...]).astype(BF)
    remote(zs, zr, ts, tr, g, tensor_of(1)).start()

    @pl.when(yh == c)
    def _():
        arrived(gb.at[0:7, x], b1r)
        for k in (6, 2, 5, 7, 4, 1, 3):
            yh_, x_ = xy_peer(k)
            remote(gb.at[:, x], gb.at[:, x], b2s, b2r, group_of(yh_, z, x_), t).start()

    arrived(uu.at[0:7], c2r)
    gathered = uu[...].reshape(128, 128)
    ups = []
    for i in range(2):
        up = jnp.where(up_lanes, dot(pu[i], gathered), 0.0)
        up = up + pltpu.roll(up, 64, 1)
        up = up + pltpu.roll(up, 32, 1)
        ups.append((up[:, 0:16].astype(BF), pltpu.roll(up, 112, 1)[:, 0:16].astype(BF)))
    arrived(uo.at[0:7], d2r)
    gathered = uo[...].reshape(256, 128)
    for h in range(8):
        dm[h * 128 : h * 128 + 128, :] = jnp.where(down_lanes, dot(pm[h], gathered), 0.0).astype(BF)
    arrived(zr, tr)
    z_key = jnp.where(c == 0, zs[...], zr[...])
    z_value = jnp.where(c == 0, zr[...], zs[...])
    key = base[0:32, :] + ADAPTER_SCALE * (dot_nt(z_key[0:32], ups[0][0]) + dot_nt(z_key[32:64], ups[0][1]))
    value = base[32:64, :] + ADAPTER_SCALE * (dot_nt(z_value[0:32], ups[1][0]) + dot_nt(z_value[32:64], ups[1][1]))
    key = (key * cosine + pltpu.roll(key, 64, 1) * sine).astype(BF)
    value = value.astype(BF)
    nk[...] = key.astype(F32)
    nv[...] = value.astype(F32)
    first_step = lax.broadcasted_iota(jnp.int32, (16, 128), 0) < 8
    for r in range(16):
        query = qs[r]
        s0 = jnp.sum(query * nk[r : r + 1, :], axis=1, keepdims=True) * SCALE
        s1 = jnp.sum(query * nk[16 + r : 17 + r, :], axis=1, keepdims=True) * SCALE
        s0 = jnp.broadcast_to(s0, (16, 128))
        s1 = jnp.where(first_step, MASKED, jnp.broadcast_to(s1, (16, 128)))
        top = jnp.maximum(mm[r], jnp.maximum(s0, s1))
        alpha = jnp.exp(mm[r] - top)
        p0 = jnp.exp(s0 - top)
        p1 = jnp.exp(s1 - top)
        total = alpha * ll[r] + p0 + p1
        ctxs[r * 16 : r * 16 + 16, :] = (alpha * acc[r] + p0 * nv[r : r + 1, :] + p1 * nv[16 + r : 17 + r, :]) / total
    for s in range(2):
        for h in range(8):
            ctx[s * 16 : s * 16 + 16, h * 128 : h * 128 + 128] = ctxs[pl.ds(s * 8 + h, 16, stride=16), :].astype(BF)

    context = ctx[...]

    l_w.wait()
    core_peer = tensor_of(1)
    chip_peer = tensor_of(2)

    def part(ref, j):
        return ref.at[:, pl.ds(pl.multiple_of(j * WIDTH, WIDTH), WIDTH)]

    def columns(half, j):
        return pl.ds(pl.multiple_of(half * 2048 + j * WIDTH, WIDTH), WIDTH)

    def give_copy(j):
        return remote(part(ps, j), part(pr, j), pss, prs.at[j], g, core_peer)

    def chip_copy(j):
        return remote(part(ys, j), part(yr, j), yss, yrs.at[j], g, chip_peer)

    def final_copy(j):
        return remote(part(fs, j), att_hbm.at[:, columns(c, j)], fss, frs, g, core_peer)

    def local_copy(j):
        return pltpu.make_async_copy(part(fs, j), att_hbm.at[:, columns(c, j)], outs)

    def give(j, _):
        part(ps, j)[...] = dot(context, w[:, columns(1 - c, j)]).astype(BF)
        give_copy(j).start()
        return 0

    def keep(j, _):
        total = dot(context, w[:, columns(c, j)])
        give_copy(j).wait_recv()
        part(ys, j)[...] = (total + part(pr, j)[...].astype(F32)).astype(BF)
        chip_copy(j).start()
        return 0

    def finish(j, _):
        term = dot(low_sum, part(u, j)[...])
        chip_copy(j).wait_recv()
        part(fs, j)[...] = ((part(ys, j)[...].astype(F32) + part(yr, j)[...].astype(F32)) + term).astype(BF)
        final_copy(j).start()
        local_copy(j).start()
        return 0

    lax.fori_loop(0, 2048 // WIDTH, give, 0)

    for s in range(2):
        nst[s, 0] = key[s * 16 : s * 16 + 16]
        nst[s, 1] = value[s * 16 : s * 16 + 16]
    l_nkv = pltpu.make_async_copy(nst, nkv_hbm, outk)
    l_nkv.start()

    low = dot(context, dm[...])
    low = low + pltpu.roll(low, 64, 1)
    low = low + pltpu.roll(low, 32, 1)
    lane8 = lax.broadcasted_iota(jnp.int32, (8, 128), 1)
    zos[...] = jnp.where(
        lane8 < 64,
        jnp.where(lane8 < 32, low[0:8], low[8:16]),
        jnp.where(lane8 < 96, low[16:24], low[24:32]),
    )
    for k in (2, 3, 1):
        remote(zos, zor.at[k], os, orr, g, tensor_of(k)).start()

    lax.fori_loop(0, 2048 // WIDTH, keep, 0)

    @pl.when(yh == c)
    def _():
        arrived(gb.at[:, 0:3], b2r)

    @pl.when(yh != c)
    def _():
        arrived(gb, b2r)

    for a in range(16):
        even = gb[a // 2, 2 * (a % 2)].astype(F32)
        odd = gb[a // 2, 2 * (a % 2) + 1].astype(F32)
        u[64:80, a * 128 : a * 128 + 128] = jnp.where(lane16 < 64, even, pltpu.roll(odd, 64, 1)).astype(BF)
        u[80:96, a * 128 : a * 128 + 128] = jnp.where(lane16 < 64, pltpu.roll(even, 64, 1), odd).astype(BF)
    arrived(zor.at[1:4], orr)
    low = (zos[...] + zor[1]) + (zor[2] + zor[3])
    low_sum = jnp.concatenate([pltpu.roll(low, 64, 1), pltpu.roll(low, 32, 1), low, pltpu.roll(low, 96, 1)], axis=0)
    low_sum = jnp.where(jnp.logical_and(lane >= 64, lane < 96), ADAPTER_SCALE * low_sum, 0.0).astype(BF)
    lax.fori_loop(0, 2048 // WIDTH, finish, 0)

    left(r1.at[0:7], a1s)
    left(gt.at[:, 0:7168], a2s)
    left(uu.at[0:7], c2s)
    left(uo.at[0:7], d2s)
    left(zs, ts)
    left(zor.at[1:4], os)
    left(ps, pss)
    left(ys, yss)
    left(fs, fss)

    @pl.when(yh == c)
    def _():
        left(gb.at[0:7, x], b1s)
        left(gt.at[:, 0:7168], b2s)

    l_nkv.wait()
    pltpu.make_async_copy(fs, fs, outs).wait()
    arrived(fs, frs)


def store(att_in, nkv_in, att_out, nkv_out, sems):
    first = pltpu.make_async_copy(att_in, att_out, sems.at[0])
    second = pltpu.make_async_copy(nkv_in, nkv_out, sems.at[1])
    first.start()
    second.start()
    first.wait()
    second.wait()


def local(hidden, queries, kv_cache, lengths, frozen_key_value, frozen_output_weight, down_kv, up_kv, down_o, up_o):
    hbm = pl.BlockSpec(memory_space=pltpu.HBM)
    dma = pltpu.SemaphoreType.DMA
    args = (
        hidden.reshape(32, 4096),
        queries,
        kv_cache.reshape(32, 256, 128),
        lengths,
        frozen_key_value.reshape(8192, 128),
        frozen_output_weight,
        down_kv.transpose(1, 2, 0).reshape(64, 64),
        up_kv.transpose(0, 2, 3, 1).reshape(2, 2, 32),
        down_o,
        up_o,
    )
    args = tuple(pltpu.with_memory_space_constraint(a, pltpu.HBM) for a in args)
    v = pltpu.VMEM
    attended, new_kv = pl.pallas_call(
        kernel,
        out_shape=(pltpu.VMEM((32, 4096), BF), pltpu.VMEM((2, 2, 16, 128), BF)),
        in_specs=[hbm] * 10,
        out_specs=(hbm, hbm),
        scratch_shapes=[
            v((32, 4096), BF), v((2, 16, 8, 128), BF), v((32, 256, 128), BF), v((8192, 128), BF), v((1024, 4096), BF),
            v((32, 64), BF), v((2, 2, 32), BF), v((8, 2, 32), BF), v((32, 64), BF),
            v((64, 8192), BF), v((16, 16, 128), F32), v((8, 2, 16, 128), BF), v((8, 4, 16, 128), BF),
            v((16, 8192), BF), v((8, 16, 128), BF), v((8, 32, 128), BF), v((64, 8192), BF), v((2, 128, 128), BF), v((8, 128, 256), BF), v((1024, 128), BF),
            v((16, 32), F32), v((16, 32), F32),
            v((64, 16), BF), v((64, 16), BF), v((8, 128), F32), v((4, 8, 128), F32),
            v((16, 16, 128), F32), v((16, 16, 128), F32), v((16, 16, 128), F32), v((256, 128), F32),
            v((32, 1024), BF), v((128, 2048), BF),
            v((32, 2048), BF), v((32, 2048), BF), v((32, 2048), BF), v((32, 2048), BF), v((32, 2048), BF),
            v((32, 128), F32), v((32, 128), F32), v((2, 2, 16, 128), BF), v((64, 128), F32), pltpu.SMEM((16,), jnp.int32),
            dma((10,)), dma((22,)), dma((2048 // WIDTH,)), dma((2048 // WIDTH,)),
        ],
        compiler_params=pltpu.CompilerParams(
            collective_id=0, has_side_effects=True, vmem_limit_bytes=40 * 1024 * 1024
        ),
    )(*args)
    attended, new_kv = pl.pallas_call(
        store,
        out_shape=(pltpu.HBM((32, 4096), BF), pltpu.HBM((2, 2, 16, 128), BF)),
        in_specs=[hbm, hbm],
        out_specs=(hbm, hbm),
        scratch_shapes=[dma((2,))],
    )(pltpu.with_memory_space_constraint(attended, pltpu.VMEM), pltpu.with_memory_space_constraint(new_kv, pltpu.VMEM))
    return attended.reshape(2, 16, 4096), new_kv.reshape(2, 2, 16, 1, 128)


def solution(mesh):
    placed = (
        P(None, "group", None),
        P(None, "group", "tensor", None),
        P(None, "group", "tensor", None, None),
        P("group"),
        P(None, None, "tensor"),
        P("tensor", None),
        P("group", None, None),
        P(None, None, "tensor", "group"),
        P("tensor", "group", None),
        P(None, "group"),
    )
    return jax.shard_map(
        local,
        mesh=mesh,
        in_specs=placed,
        out_specs=(P(None, "group", None), P(None, None, "group", "tensor", None)),
        check_vma=False,
    )
```

```python
import math

import jax
import jax.numpy as jnp
from jax import lax
from jax.experimental import pallas as pl
from jax.experimental.pallas import tpu as pltpu
from jax.sharding import PartitionSpec as P

BF = jnp.bfloat16
F32 = jnp.float32
MESH = pl.DeviceIdType.MESH

ADAPTER_SCALE = 2.0
ROPE_BASE = 500000.0
SCALE = 1.0 / math.sqrt(128.0)
MASKED = -1e30
WIDTH = 512

NT = (((1,), (1,)), ((), ()))


def dot(a, b):
    return jnp.dot(a, b, preferred_element_type=F32)


def dot_nt(a, b):
    return lax.dot_general(a, b, NT, preferred_element_type=F32)


def place(rows, columns, offset):
    i = lax.broadcasted_iota(jnp.int32, (rows, columns), 0)
    j = lax.broadcasted_iota(jnp.int32, (rows, columns), 1)
    return jnp.where(j == i + offset, 1.0, 0.0).astype(BF)


def kernel(
    hid_hbm, q_hbm, kv_hbm, len_hbm, fkv_hbm, w_hbm, dkv_hbm, ukv_hbm, do_hbm, uo_hbm,
    att_hbm, nkv_hbm,
    hid, q_v, kv, fkv, w, dk_v, uk_v, do_v, uo_v,
    hx, qs, r1, gb, gt, uo, hd, pu, pm, dm, s16, s4,
    zs, zr, zos, zor, acc, mm, ll, ctxs, ctx, u,
    ps, pr, ys, yr, fs, nk, nv, nst, base, sc, pe, len_ref,
    lsem, one, prs, yrs, came,
):
    a1s, a1r, a2s, a2r, b1s, b1r, b2s, b2r, ts, tr, os, orr, pss, yss, fss, frs, outs, outk, c2s, c2r = (one.at[i] for i in range(20))
    g = lax.axis_index("group")
    t = lax.axis_index("tensor")
    yh = lax.div(g, 32)
    z = lax.rem(lax.div(g, 4), 8)
    x = lax.rem(g, 4)
    yl = lax.div(t, 2)
    c = lax.rem(t, 2)

    def group_of(yh_, z_, x_):
        return yh_ * 32 + z_ * 4 + x_

    def tensor_of(k):
        yl_ = yl if k < 2 else 1 - yl
        c_ = c if k % 2 == 0 else 1 - c
        return yl_ * 2 + c_

    def remote(src, dst, ss, rs, group, tensor):
        return pltpu.make_async_remote_copy(
            src_ref=src, dst_ref=dst, send_sem=ss, recv_sem=rs,
            device_id={"group": group, "tensor": tensor}, device_id_type=MESH,
        )

    barrier = pltpu.get_barrier_semaphore()

    def xy_peer(k):
        return (yh if k < 4 else 1 - yh), lax.rem(x + k % 4, 4)

    def arrived(ref, sem):
        remote(ref, ref, ts, sem, g, t).wait_recv()

    def left(ref, sem):
        remote(ref, ref, sem, tr, g, t).wait_send()

    def load(src, dst, i):
        copy = pltpu.make_async_copy(src, dst, lsem.at[i])
        copy.start()
        return copy

    l_dk = load(dkv_hbm.at[pl.ds(pl.multiple_of(c * 32, 32), 32), :], dk_v, 0)
    l_uk = load(ukv_hbm, uk_v, 1)
    l_do = load(do_hbm, do_v, 2)
    l_uo = load(uo_hbm, uo_v, 3)

    def greet(group, tensor):
        pl.semaphore_signal(barrier, inc=1, device_id={"group": group, "tensor": tensor}, device_id_type=MESH)

    for hop, k in (
        ("xy", 6), ("z", 4), ("z", 3), ("z", 5), ("xy", 5), ("xy", 7), ("xy", 2), ("z", 2), ("z", 6),
        ("xy", 4), ("xy", 1), ("xy", 3), ("z", 1), ("z", 7), ("t", 2), ("t", 3), ("t", 1),
    ):
        if hop == "z":
            greet(group_of(yh, lax.rem(z + k, 8), x), t)
        elif hop == "xy":
            greet(group_of(xy_peer(k)[0], z, xy_peer(k)[1]), t)
        else:
            greet(g, tensor_of(k))

    l_hid = load(hid_hbm, hid, 4)
    l_q = load(q_hbm, q_v, 5)
    l_fkv = load(fkv_hbm, fkv, 6)
    l_kv = load(kv_hbm, kv, 7)
    l_len = load(len_hbm, len_ref, 9)
    l_w = load(w_hbm, w, 8)

    m = lax.rem(z, 4)
    q = lax.rem(m + jnp.where(z < 4, 1, 2), 4)
    l_dk.wait()
    l_uk.wait()
    l_do.wait()
    for h in range(8):
        s16[2 * h : 2 * h + 2, :] = do_v[h].astype(F32)
    for k in range(2):
        for i in range(4):
            s4[4 * i + 2 * k : 4 * i + 2 * k + 2, :] = uk_v[k].astype(F32)
    row16 = lax.broadcasted_iota(jnp.int32, (16, 32), 0)
    up_rows = jnp.where(jnp.logical_and(row16 >= 4 * m, row16 < 4 * m + 4), s4[...], 0.0)
    half = dk_v[...]
    r1[z, 0] = (dot(half[0:16], place(64, 128, 0)) + dot(half[16:32], place(64, 128, 64))).astype(BF)
    r1[z, 1] = (
        dot(s16[...].astype(BF), place(32, 128, 32 * m)) + dot(up_rows.astype(BF), place(32, 128, 32 * q))
    ).astype(BF)
    l_uo.wait()

    @pl.when(yh == c)
    def _():
        up = uo_v[...]
        gb[z, x] = (dot(up[0:16], place(64, 128, 0)) + dot(up[16:32], place(64, 128, 64))).astype(BF)

    lane = lax.broadcasted_iota(jnp.int32, (32, 128), 1)
    pl.semaphore_wait(barrier, 17)

    for k in (4, 3, 5, 2, 6, 1, 7):
        remote(r1.at[z], r1.at[z], a1s, a1r, group_of(yh, lax.rem(z + k, 8), x), t).start()

    feature = lax.broadcasted_iota(jnp.int32, (128, 256), 0)
    source = lax.broadcasted_iota(jnp.int32, (128, 256), 1)

    def digit(value, shift, mask):
        return jnp.bitwise_and(lax.shift_right_logical(value, shift), mask)

    tile = digit(feature, 6, 1) * 4 + digit(feature, 1, 3)
    from_up = (tile * 16 + 4 * digit(feature, 3, 3) + digit(feature, 0, 1))[:, :128]
    from_down = tile * 32 + 16 * digit(feature, 5, 1) + digit(feature, 0, 1)
    for i in range(2):
        pu[i] = jnp.where(source[:, :128] == from_up + 2 * i, 1.0, 0.0).astype(BF)
    for h in range(8):
        pm[h] = jnp.where(source == from_down + 2 * h, 1.0, 0.0).astype(BF)
    square = lax.broadcasted_iota(jnp.int32, (128, 128), 0)
    lane_group = digit(lax.broadcasted_iota(jnp.int32, (128, 128), 1), 5, 3)
    up_lanes = lane_group == digit(digit(square, 3, 3) + 1 + digit(square, 5, 1), 0, 3)
    down_lanes = lane_group == digit(square, 3, 3)

    l_len.wait()
    sub = lax.broadcasted_iota(jnp.int32, (32, 128), 0)
    later = jnp.where(sub >= 16, 1, 0)
    in_step = sub - 16 * later
    position = later
    for r in range(16):
        position = position + jnp.where(in_step == r, len_ref[r], 0)
    counter = jnp.where(lane < 64, lane, lane - 64).astype(F32)
    angle = position.astype(F32) * jnp.exp(counter * (-2.0 * math.log(ROPE_BASE) / 128))
    cosine = jnp.cos(angle)
    sine = jnp.sin(angle)
    sine = jnp.where(lane < 64, -sine, sine)

    l_hid.wait()
    row = lax.broadcasted_iota(jnp.int32, (128, 512), 0)
    col = lax.broadcasted_iota(jnp.int32, (128, 512), 1)
    spread = jnp.where(jnp.where(col < 256, col, col - 257) == 2 * row, 1.0, 0.0).astype(BF)

    def spread_chunk(a, _):
        part = dot(hid[:, pl.ds(pl.multiple_of(a * 128, 128), 128)], spread).astype(BF)
        at = pl.ds(pl.multiple_of(a * 256, 256), 256)
        hx[0:32, at] = part[:, :256]
        hx[32:64, at] = part[:, 256:]
        return 0

    lax.fori_loop(0, 32, spread_chunk, 0, unroll=8)

    for a in range(32):
        pair = hid[:, a * 128 : a * 128 + 128].astype(F32)
        turned = pltpu.roll(pair, 64, 1)
        at = ((a // 16) * 4 + 2 * (a % 2)) * 1024 + (a // 2 % 8) * 128
        hd[0:32, at : at + 128] = jnp.where(lane < 64, pair, 0.0).astype(BF)
        hd[32:64, at : at + 128] = jnp.where(lane < 64, 0.0, turned).astype(BF)
        at = at + 1024
        hd[0:32, at : at + 128] = jnp.where(lane < 64, turned, 0.0).astype(BF)
        hd[32:64, at : at + 128] = jnp.where(lane < 64, 0.0, pair).astype(BF)

    l_fkv.wait()

    def project(a, total):
        at = pl.ds(pl.multiple_of(a * 1024, 1024), 1024)
        return total + dot(hx[:, at], fkv[at, :])

    base[...] = lax.fori_loop(0, 8, project, jnp.zeros((64, 128), F32), unroll=4)

    l_q.wait()
    for s in range(2):
        qs[:, s * 8 : s * 8 + 8, :] = q_v[s].astype(F32)
    l_kv.wait()
    for r in range(16):
        sc[r] = dot_nt(qs[r].astype(BF), kv[r])

    slots = lax.broadcasted_iota(jnp.int32, (16, 256), 1)
    for r in range(16):
        scores = jnp.where(slots < len_ref[r], sc[r] * SCALE, MASKED)
        top = jnp.max(scores, axis=1, keepdims=True)
        expo = jnp.exp(scores - top)
        pe[r] = expo.astype(BF)
        mm[r] = jnp.broadcast_to(top, (16, 128))
        ll[r] = jnp.broadcast_to(jnp.sum(expo, axis=1, keepdims=True), (16, 128))
    for r in range(16):
        acc[r] = dot(pe[r], kv[16 + r])
    u[...] = jnp.zeros_like(u)

    lane16 = lax.broadcasted_iota(jnp.int32, (16, 128), 1)
    block = yh * 4 + x
    arrived(r1.at[0:7], a1r)
    for z_ in range(8):
        gt[:, pl.ds(pl.multiple_of(block * 1024 + z_ * 128, 128), 128)] = r1[z_, 0]
    own_lanes = gt.at[:, pl.ds(pl.multiple_of(block * 1024, 1024), 1024)]
    for k in (6, 2, 5, 7, 4, 1, 3):
        yh_, x_ = xy_peer(k)
        remote(own_lanes, own_lanes, a2s, came.at[k], group_of(yh_, z, x_), t).start()
    others = [r1[z_, 1].astype(F32) for z_ in range(8)]

    def lanes_of(z_, i):
        return jnp.where(jnp.logical_and(lane16 >= 32 * i, lane16 < 32 * i + 32), others[z_], 0.0)

    uo[block, 0:16] = sum(lanes_of(z_, (z_ % 4 + 1 + z_ // 4) % 4) for z_ in range(8)).astype(BF)
    uo[block, 16:32] = sum(lanes_of(z_, z_) for z_ in range(4)).astype(BF)
    uo[block, 32:48] = sum(lanes_of(z_, z_ - 4) for z_ in range(4, 8)).astype(BF)
    for k in (6, 2, 5, 7, 4, 1, 3):
        yh_, x_ = xy_peer(k)
        remote(uo.at[block], uo.at[block], c2s, c2r, group_of(yh_, z, x_), t).start()

    @pl.when(yh == c)
    def _():
        for k in (4, 3, 5, 2, 6, 1, 7):
            remote(gb.at[z, x], gb.at[z, x], b1s, b1r, group_of(yh, lax.rem(z + k, 8), x), t).start()


    def down_part(from_block):
        at = pl.ds(pl.multiple_of(from_block * 1024, 1024), 1024)
        return dot_nt(hd[:, at], gt[:, at])

    low = down_part(block)
    for k in (1, 3, 4, 2, 7, 5, 6):
        from_block = (yh if k < 4 else 1 - yh) * 4 + lax.rem(x + 4 - k % 4, 4)
        arrived(gt.at[:, pl.ds(pl.multiple_of(from_block * 1024, 1024), 1024)], came.at[k])
        low = low + down_part(from_block)
    zs[...] = low.astype(BF)
    remote(zs, zr, ts, tr, g, tensor_of(1)).start()

    @pl.when(yh == c)
    def _():
        arrived(gb.at[0:7, x], b1r)
        for k in (6, 2, 5, 7, 4, 1, 3):
            yh_, x_ = xy_peer(k)
            remote(gb.at[:, x], gb.at[:, x], b2s, b2r, group_of(yh_, z, x_), t).start()

    arrived(uo.at[0:7], c2r)
    gathered = uo[:, 0:16].reshape(128, 128)
    ups = []
    for i in range(2):
        up = jnp.where(up_lanes, dot(pu[i], gathered), 0.0)
        up = up + pltpu.roll(up, 64, 1)
        up = up + pltpu.roll(up, 32, 1)
        ups.append((up[:, 0:16].astype(BF), pltpu.roll(up, 112, 1)[:, 0:16].astype(BF)))
    gathered = uo[:, 16:48].reshape(256, 128)
    for h in range(8):
        dm[h * 128 : h * 128 + 128, :] = jnp.where(down_lanes, dot(pm[h], gathered), 0.0).astype(BF)
    arrived(zr, tr)
    z_key = jnp.where(c == 0, zs[...], zr[...])
    z_value = jnp.where(c == 0, zr[...], zs[...])
    key = base[0:32, :] + ADAPTER_SCALE * (dot_nt(z_key[0:32], ups[0][0]) + dot_nt(z_key[32:64], ups[0][1]))
    value = base[32:64, :] + ADAPTER_SCALE * (dot_nt(z_value[0:32], ups[1][0]) + dot_nt(z_value[32:64], ups[1][1]))
    key = (key * cosine + pltpu.roll(key, 64, 1) * sine).astype(BF)
    value = value.astype(BF)
    nk[...] = key.astype(F32)
    nv[...] = value.astype(F32)
    first_step = lax.broadcasted_iota(jnp.int32, (16, 128), 0) < 8
    for r in range(16):
        query = qs[r]
        s0 = jnp.sum(query * nk[r : r + 1, :], axis=1, keepdims=True) * SCALE
        s1 = jnp.sum(query * nk[16 + r : 17 + r, :], axis=1, keepdims=True) * SCALE
        s0 = jnp.broadcast_to(s0, (16, 128))
        s1 = jnp.where(first_step, MASKED, jnp.broadcast_to(s1, (16, 128)))
        top = jnp.maximum(mm[r], jnp.maximum(s0, s1))
        alpha = jnp.exp(mm[r] - top)
        p0 = jnp.exp(s0 - top)
        p1 = jnp.exp(s1 - top)
        total = alpha * ll[r] + p0 + p1
        ctxs[r * 16 : r * 16 + 16, :] = (alpha * acc[r] + p0 * nv[r : r + 1, :] + p1 * nv[16 + r : 17 + r, :]) / total
    for s in range(2):
        for h in range(8):
            ctx[s * 16 : s * 16 + 16, h * 128 : h * 128 + 128] = ctxs[pl.ds(s * 8 + h, 16, stride=16), :].astype(BF)

    context = ctx[...]

    l_w.wait()
    core_peer = tensor_of(1)
    chip_peer = tensor_of(2)

    def part(ref, j):
        return ref.at[:, pl.ds(pl.multiple_of(j * WIDTH, WIDTH), WIDTH)]

    def columns(half, j):
        return pl.ds(pl.multiple_of(half * 2048 + j * WIDTH, WIDTH), WIDTH)

    def give_copy(j):
        return remote(part(ps, j), part(pr, j), pss, prs.at[j], g, core_peer)

    def chip_copy(j):
        return remote(part(ys, j), part(yr, j), yss, yrs.at[j], g, chip_peer)

    def final_copy(j):
        return remote(part(fs, j), att_hbm.at[:, columns(c, j)], fss, frs, g, core_peer)

    def local_copy(j):
        return pltpu.make_async_copy(part(fs, j), att_hbm.at[:, columns(c, j)], outs)

    def give(j, _):
        part(ps, j)[...] = dot(context, w[:, columns(1 - c, j)]).astype(BF)
        give_copy(j).start()
        return 0

    def keep(j, _):
        total = dot(context, w[:, columns(c, j)])
        give_copy(j).wait_recv()
        part(ys, j)[...] = (total + part(pr, j)[...].astype(F32)).astype(BF)
        chip_copy(j).start()
        return 0

    def finish(j, _):
        term = dot(low_sum, part(u, j)[...])
        chip_copy(j).wait_recv()
        part(fs, j)[...] = ((part(ys, j)[...].astype(F32) + part(yr, j)[...].astype(F32)) + term).astype(BF)
        final_copy(j).start()
        local_copy(j).start()
        return 0

    lax.fori_loop(0, 2048 // WIDTH, give, 0)

    for s in range(2):
        nst[s, 0] = key[s * 16 : s * 16 + 16]
        nst[s, 1] = value[s * 16 : s * 16 + 16]
    l_nkv = pltpu.make_async_copy(nst, nkv_hbm, outk)
    l_nkv.start()

    low = dot(context, dm[...])
    low = low + pltpu.roll(low, 64, 1)
    low = low + pltpu.roll(low, 32, 1)
    lane8 = lax.broadcasted_iota(jnp.int32, (8, 128), 1)
    zos[...] = jnp.where(
        lane8 < 64,
        jnp.where(lane8 < 32, low[0:8], low[8:16]),
        jnp.where(lane8 < 96, low[16:24], low[24:32]),
    )
    for k in (2, 3, 1):
        remote(zos, zor.at[k], os, orr, g, tensor_of(k)).start()

    lax.fori_loop(0, 2048 // WIDTH, keep, 0)

    @pl.when(yh == c)
    def _():
        arrived(gb.at[:, 0:3], b2r)

    @pl.when(yh != c)
    def _():
        arrived(gb, b2r)

    for a in range(16):
        even = gb[a // 2, 2 * (a % 2)].astype(F32)
        odd = gb[a // 2, 2 * (a % 2) + 1].astype(F32)
        u[64:80, a * 128 : a * 128 + 128] = jnp.where(lane16 < 64, even, pltpu.roll(odd, 64, 1)).astype(BF)
        u[80:96, a * 128 : a * 128 + 128] = jnp.where(lane16 < 64, pltpu.roll(even, 64, 1), odd).astype(BF)
    arrived(zor.at[1:4], orr)
    low = (zos[...] + zor[1]) + (zor[2] + zor[3])
    low_sum = jnp.concatenate([pltpu.roll(low, 64, 1), pltpu.roll(low, 32, 1), low, pltpu.roll(low, 96, 1)], axis=0)
    low_sum = jnp.where(jnp.logical_and(lane >= 64, lane < 96), ADAPTER_SCALE * low_sum, 0.0).astype(BF)
    lax.fori_loop(0, 2048 // WIDTH, finish, 0)

    left(r1.at[0:7], a1s)
    left(gt.at[:, 0:7168], a2s)
    left(uo.at[0:7], c2s)
    left(zs, ts)
    left(zor.at[1:4], os)
    left(ps, pss)
    left(ys, yss)
    left(fs, fss)

    @pl.when(yh == c)
    def _():
        left(gb.at[0:7, x], b1s)
        left(gt.at[:, 0:7168], b2s)

    l_nkv.wait()
    pltpu.make_async_copy(fs, fs, outs).wait()
    arrived(fs, frs)


def store(att_in, nkv_in, att_out, nkv_out, sems):
    first = pltpu.make_async_copy(att_in, att_out, sems.at[0])
    second = pltpu.make_async_copy(nkv_in, nkv_out, sems.at[1])
    first.start()
    second.start()
    first.wait()
    second.wait()


def local(hidden, queries, kv_cache, lengths, frozen_key_value, frozen_output_weight, down_kv, up_kv, down_o, up_o):
    hbm = pl.BlockSpec(memory_space=pltpu.HBM)
    dma = pltpu.SemaphoreType.DMA
    args = (
        hidden.reshape(32, 4096),
        queries,
        kv_cache.reshape(32, 256, 128),
        lengths,
        frozen_key_value.reshape(8192, 128),
        frozen_output_weight,
        down_kv.transpose(1, 2, 0).reshape(64, 64),
        up_kv.transpose(0, 2, 3, 1).reshape(2, 2, 32),
        down_o,
        up_o,
    )
    args = tuple(pltpu.with_memory_space_constraint(a, pltpu.HBM) for a in args)
    v = pltpu.VMEM
    attended, new_kv = pl.pallas_call(
        kernel,
        out_shape=(pltpu.VMEM((32, 4096), BF), pltpu.VMEM((2, 2, 16, 128), BF)),
        in_specs=[hbm] * 10,
        out_specs=(hbm, hbm),
        scratch_shapes=[
            v((32, 4096), BF), v((2, 16, 8, 128), BF), v((32, 256, 128), BF), v((8192, 128), BF), v((1024, 4096), BF),
            v((32, 64), BF), v((2, 2, 32), BF), v((8, 2, 32), BF), v((32, 64), BF),
            v((64, 8192), BF), v((16, 16, 128), F32), v((8, 2, 16, 128), BF), v((8, 4, 16, 128), BF),
            v((16, 8192), BF), v((8, 48, 128), BF), v((64, 8192), BF), v((2, 128, 128), BF), v((8, 128, 256), BF), v((1024, 128), BF),
            v((16, 32), F32), v((16, 32), F32),
            v((64, 16), BF), v((64, 16), BF), v((8, 128), F32), v((4, 8, 128), F32),
            v((16, 16, 128), F32), v((16, 16, 128), F32), v((16, 16, 128), F32), v((256, 128), F32),
            v((32, 1024), BF), v((128, 2048), BF),
            v((32, 2048), BF), v((32, 2048), BF), v((32, 2048), BF), v((32, 2048), BF), v((32, 2048), BF),
            v((32, 128), F32), v((32, 128), F32), v((2, 2, 16, 128), BF), v((64, 128), F32), v((16, 16, 256), F32), v((16, 16, 256), BF), pltpu.SMEM((16,), jnp.int32),
            dma((10,)), dma((20,)), dma((2048 // WIDTH,)), dma((2048 // WIDTH,)), dma((8,)),
        ],
        compiler_params=pltpu.CompilerParams(
            collective_id=0, has_side_effects=True, vmem_limit_bytes=40 * 1024 * 1024
        ),
    )(*args)
    attended, new_kv = pl.pallas_call(
        store,
        out_shape=(pltpu.HBM((32, 4096), BF), pltpu.HBM((2, 2, 16, 128), BF)),
        in_specs=[hbm, hbm],
        out_specs=(hbm, hbm),
        scratch_shapes=[dma((2,))],
    )(pltpu.with_memory_space_constraint(attended, pltpu.VMEM), pltpu.with_memory_space_constraint(new_kv, pltpu.VMEM))
    return attended.reshape(2, 16, 4096), new_kv.reshape(2, 2, 16, 1, 128)


def solution(mesh):
    placed = (
        P(None, "group", None),
        P(None, "group", "tensor", None),
        P(None, "group", "tensor", None, None),
        P("group"),
        P(None, None, "tensor"),
        P("tensor", None),
        P("group", None, None),
        P(None, None, "tensor", "group"),
        P("tensor", "group", None),
        P(None, "group"),
    )
    return jax.shard_map(
        local,
        mesh=mesh,
        in_specs=placed,
        out_specs=(P(None, "group", None), P(None, None, "group", "tensor", None)),
        check_vma=False,
    )
```

```python
import math

import jax
import jax.numpy as jnp
from jax import lax
from jax.experimental import pallas as pl
from jax.experimental.pallas import tpu as pltpu
from jax.sharding import PartitionSpec as P

BF = jnp.bfloat16
F32 = jnp.float32
MESH = pl.DeviceIdType.MESH

ADAPTER_SCALE = 2.0
ROPE_BASE = 500000.0
SCALE = 1.0 / math.sqrt(128.0)
MASKED = -1e30
WIDTH = 512

NT = (((1,), (1,)), ((), ()))


def dot(a, b):
    return jnp.dot(a, b, preferred_element_type=F32)


def dot_nt(a, b):
    return lax.dot_general(a, b, NT, preferred_element_type=F32)


def place(rows, columns, offset):
    i = lax.broadcasted_iota(jnp.int32, (rows, columns), 0)
    j = lax.broadcasted_iota(jnp.int32, (rows, columns), 1)
    return jnp.where(j == i + offset, 1.0, 0.0).astype(BF)


def kernel(
    hid_hbm, q_hbm, kv_hbm, len_hbm, fkv_hbm, w_hbm, dkv_hbm, ukv_hbm, do_hbm, uo_hbm,
    att_hbm, nkv_hbm,
    hid, q_v, kv, fkv, w, dk_v, uk_v, do_v, uo_v,
    hx, qs, r1, gb, gt, uo, hd, pu, pm, dm, s16, s4,
    zs, zr, zos, zor, acc, mm, ll, ctxs, ctx, u,
    ps, pr, ys, yr, fs, nk, nv, nst, base, sc, pe, len_ref,
    lsem, one, prs, yrs, came,
):
    a1s, a1r, a2s, a2r, b1s, b1r, b2s, b2r, ts, tr, os, orr, pss, yss, fss, frs, outs, outk, c2s, c2r = (one.at[i] for i in range(20))
    g = lax.axis_index("group")
    t = lax.axis_index("tensor")
    yh = lax.div(g, 32)
    z = lax.rem(lax.div(g, 4), 8)
    x = lax.rem(g, 4)
    yl = lax.div(t, 2)
    c = lax.rem(t, 2)

    def group_of(yh_, z_, x_):
        return yh_ * 32 + z_ * 4 + x_

    def tensor_of(k):
        yl_ = yl if k < 2 else 1 - yl
        c_ = c if k % 2 == 0 else 1 - c
        return yl_ * 2 + c_

    def remote(src, dst, ss, rs, group, tensor):
        return pltpu.make_async_remote_copy(
            src_ref=src, dst_ref=dst, send_sem=ss, recv_sem=rs,
            device_id={"group": group, "tensor": tensor}, device_id_type=MESH,
        )

    barrier = pltpu.get_barrier_semaphore()

    def xy_peer(k):
        return (yh if k < 4 else 1 - yh), lax.rem(x + k % 4, 4)

    def arrived(ref, sem):
        remote(ref, ref, ts, sem, g, t).wait_recv()

    def left(ref, sem):
        remote(ref, ref, sem, tr, g, t).wait_send()

    def load(src, dst, i):
        copy = pltpu.make_async_copy(src, dst, lsem.at[i])
        copy.start()
        return copy

    l_dk = load(dkv_hbm.at[pl.ds(pl.multiple_of(c * 32, 32), 32), :], dk_v, 0)
    l_uk = load(ukv_hbm, uk_v, 1)
    l_do = load(do_hbm, do_v, 2)
    l_uo = load(uo_hbm, uo_v, 3)

    def greet(group, tensor):
        pl.semaphore_signal(barrier, inc=1, device_id={"group": group, "tensor": tensor}, device_id_type=MESH)

    for hop, k in (
        ("xy", 6), ("z", 4), ("z", 3), ("z", 5), ("xy", 5), ("xy", 7), ("xy", 2), ("z", 2), ("z", 6),
        ("xy", 4), ("xy", 1), ("xy", 3), ("z", 1), ("z", 7), ("t", 2), ("t", 3), ("t", 1),
    ):
        if hop == "z":
            greet(group_of(yh, lax.rem(z + k, 8), x), t)
        elif hop == "xy":
            greet(group_of(xy_peer(k)[0], z, xy_peer(k)[1]), t)
        else:
            greet(g, tensor_of(k))

    l_hid = load(hid_hbm, hid, 4)
    l_q = load(q_hbm, q_v, 5)
    l_fkv = load(fkv_hbm, fkv, 6)
    l_kv = load(kv_hbm, kv, 7)
    l_len = load(len_hbm, len_ref, 9)
    l_w = load(w_hbm, w, 8)

    m = lax.rem(z, 4)
    q = lax.rem(m + jnp.where(z < 4, 1, 2), 4)
    l_dk.wait()
    l_uk.wait()
    l_do.wait()
    for h in range(8):
        s16[2 * h : 2 * h + 2, :] = do_v[h].astype(F32)
    for k in range(2):
        for i in range(4):
            s4[4 * i + 2 * k : 4 * i + 2 * k + 2, :] = uk_v[k].astype(F32)
    row16 = lax.broadcasted_iota(jnp.int32, (16, 32), 0)
    up_rows = jnp.where(jnp.logical_and(row16 >= 4 * m, row16 < 4 * m + 4), s4[...], 0.0)
    half = dk_v[...]
    r1[z, 0] = (dot(half[0:16], place(64, 128, 0)) + dot(half[16:32], place(64, 128, 64))).astype(BF)
    r1[z, 1] = (
        dot(s16[...].astype(BF), place(32, 128, 32 * m)) + dot(up_rows.astype(BF), place(32, 128, 32 * q))
    ).astype(BF)
    l_uo.wait()

    @pl.when(yh == c)
    def _():
        up = uo_v[...]
        gb[z, x] = (dot(up[0:16], place(64, 128, 0)) + dot(up[16:32], place(64, 128, 64))).astype(BF)

    lane = lax.broadcasted_iota(jnp.int32, (32, 128), 1)
    pl.semaphore_wait(barrier, 17)

    for k in (4, 3, 5, 2, 6, 1, 7):
        remote(r1.at[z], r1.at[z], a1s, a1r, group_of(yh, lax.rem(z + k, 8), x), t).start()

    feature = lax.broadcasted_iota(jnp.int32, (128, 256), 0)
    source = lax.broadcasted_iota(jnp.int32, (128, 256), 1)

    def digit(value, shift, mask):
        return jnp.bitwise_and(lax.shift_right_logical(value, shift), mask)

    tile = digit(feature, 6, 1) * 4 + digit(feature, 1, 3)
    from_up = (tile * 16 + 4 * digit(feature, 3, 3) + digit(feature, 0, 1))[:, :128]
    from_down = tile * 32 + 16 * digit(feature, 5, 1) + digit(feature, 0, 1)
    for i in range(2):
        pu[i] = jnp.where(source[:, :128] == from_up + 2 * i, 1.0, 0.0).astype(BF)
    for h in range(8):
        pm[h] = jnp.where(source == from_down + 2 * h, 1.0, 0.0).astype(BF)
    square = lax.broadcasted_iota(jnp.int32, (128, 128), 0)
    lane_group = digit(lax.broadcasted_iota(jnp.int32, (128, 128), 1), 5, 3)
    up_lanes = lane_group == digit(digit(square, 3, 3) + 1 + digit(square, 5, 1), 0, 3)
    down_lanes = lane_group == digit(square, 3, 3)

    l_len.wait()
    sub = lax.broadcasted_iota(jnp.int32, (32, 128), 0)
    later = jnp.where(sub >= 16, 1, 0)
    in_step = sub - 16 * later
    position = later
    for r in range(16):
        position = position + jnp.where(in_step == r, len_ref[r], 0)
    counter = jnp.where(lane < 64, lane, lane - 64).astype(F32)
    angle = position.astype(F32) * jnp.exp(counter * (-2.0 * math.log(ROPE_BASE) / 128))
    cosine = jnp.cos(angle)
    sine = jnp.sin(angle)
    sine = jnp.where(lane < 64, -sine, sine)

    l_hid.wait()
    row = lax.broadcasted_iota(jnp.int32, (128, 512), 0)
    col = lax.broadcasted_iota(jnp.int32, (128, 512), 1)
    spread = jnp.where(jnp.where(col < 256, col, col - 257) == 2 * row, 1.0, 0.0).astype(BF)

    def spread_chunk(a, _):
        part = dot(hid[:, pl.ds(pl.multiple_of(a * 128, 128), 128)], spread).astype(BF)
        at = pl.ds(pl.multiple_of(a * 256, 256), 256)
        hx[0:32, at] = part[:, :256]
        hx[32:64, at] = part[:, 256:]
        return 0

    lax.fori_loop(0, 32, spread_chunk, 0, unroll=8)

    for a in range(32):
        pair = hid[:, a * 128 : a * 128 + 128].astype(F32)
        turned = pltpu.roll(pair, 64, 1)
        at = ((a // 16) * 4 + 2 * (a % 2)) * 1024 + (a // 2 % 8) * 128
        hd[0:32, at : at + 128] = jnp.where(lane < 64, pair, 0.0).astype(BF)
        hd[32:64, at : at + 128] = jnp.where(lane < 64, 0.0, turned).astype(BF)
        at = at + 1024
        hd[0:32, at : at + 128] = jnp.where(lane < 64, turned, 0.0).astype(BF)
        hd[32:64, at : at + 128] = jnp.where(lane < 64, 0.0, pair).astype(BF)

    l_fkv.wait()

    def project(a, total):
        at = pl.ds(pl.multiple_of(a * 1024, 1024), 1024)
        return total + dot(hx[:, at], fkv[at, :])

    base[...] = lax.fori_loop(0, 8, project, jnp.zeros((64, 128), F32), unroll=4)

    l_q.wait()
    for s in range(2):
        qs[:, s * 8 : s * 8 + 8, :] = q_v[s].astype(F32)
    l_kv.wait()
    for r in range(16):
        sc[r] = dot_nt(qs[r].astype(BF), kv[r])

    slots = lax.broadcasted_iota(jnp.int32, (16, 256), 1)
    for r in range(16):
        scores = jnp.where(slots < len_ref[r], sc[r] * SCALE, MASKED)
        top = jnp.max(scores, axis=1, keepdims=True)
        expo = jnp.exp(scores - top)
        pe[r] = expo.astype(BF)
        mm[r] = jnp.broadcast_to(top, (16, 128))
        ll[r] = jnp.broadcast_to(jnp.sum(expo, axis=1, keepdims=True), (16, 128))
    for r in range(16):
        acc[r] = dot(pe[r], kv[16 + r])
    u[...] = jnp.zeros_like(u)

    lane16 = lax.broadcasted_iota(jnp.int32, (16, 128), 1)
    block = yh * 4 + x
    arrived(r1.at[0:7], a1r)
    for z_ in range(8):
        gt[:, pl.ds(pl.multiple_of(block * 1024 + z_ * 128, 128), 128)] = r1[z_, 0]
    own_lanes = gt.at[:, pl.ds(pl.multiple_of(block * 1024, 1024), 1024)]
    for k in (6, 2, 5, 7, 4, 1, 3):
        yh_, x_ = xy_peer(k)
        remote(own_lanes, own_lanes, a2s, came.at[k], group_of(yh_, z, x_), t).start()
    others = [r1[z_, 1].astype(F32) for z_ in range(8)]

    def lanes_of(z_, i):
        return jnp.where(jnp.logical_and(lane16 >= 32 * i, lane16 < 32 * i + 32), others[z_], 0.0)

    uo[block, 0:16] = sum(lanes_of(z_, (z_ % 4 + 1 + z_ // 4) % 4) for z_ in range(8)).astype(BF)
    uo[block, 16:32] = sum(lanes_of(z_, z_) for z_ in range(4)).astype(BF)
    uo[block, 32:48] = sum(lanes_of(z_, z_ - 4) for z_ in range(4, 8)).astype(BF)
    for k in (6, 2, 5, 7, 4, 1, 3):
        yh_, x_ = xy_peer(k)
        remote(uo.at[block], uo.at[block], c2s, c2r, group_of(yh_, z, x_), t).start()

    @pl.when(yh == c)
    def _():
        for k in (4, 3, 5, 2, 6, 1, 7):
            remote(gb.at[z, x], gb.at[z, x], b1s, b1r, group_of(yh, lax.rem(z + k, 8), x), t).start()


    def down_part(from_block):
        at = pl.ds(pl.multiple_of(from_block * 1024, 1024), 1024)
        return dot_nt(hd[:, at], gt[:, at])

    low = down_part(block)
    for k in (1, 3, 4, 2, 7, 5, 6):
        from_block = (yh if k < 4 else 1 - yh) * 4 + lax.rem(x + 4 - k % 4, 4)
        arrived(gt.at[:, pl.ds(pl.multiple_of(from_block * 1024, 1024), 1024)], came.at[k])
        low = low + down_part(from_block)
    zs[...] = low.astype(BF)
    remote(zs, zr, ts, tr, g, tensor_of(1)).start()

    @pl.when(yh == c)
    def _():
        arrived(gb.at[0:7, x], b1r)
        for k in (6, 2, 5, 7, 4, 1, 3):
            yh_, x_ = xy_peer(k)
            remote(gb.at[:, x], gb.at[:, x], b2s, b2r, group_of(yh_, z, x_), t).start()

    arrived(uo.at[0:7], c2r)
    gathered = uo[:, 0:16].reshape(128, 128)
    ups = []
    for i in range(2):
        up = jnp.where(up_lanes, dot(pu[i], gathered), 0.0)
        up = up + pltpu.roll(up, 64, 1)
        up = up + pltpu.roll(up, 32, 1)
        ups.append((up[:, 0:16].astype(BF), pltpu.roll(up, 112, 1)[:, 0:16].astype(BF)))
    gathered = uo[:, 16:48].reshape(256, 128)
    for h in range(8):
        dm[h * 128 : h * 128 + 128, :] = jnp.where(down_lanes, dot(pm[h], gathered), 0.0).astype(BF)
    arrived(zr, tr)
    z_key = jnp.where(c == 0, zs[...], zr[...])
    z_value = jnp.where(c == 0, zr[...], zs[...])
    key = base[0:32, :] + ADAPTER_SCALE * (dot_nt(z_key[0:32], ups[0][0]) + dot_nt(z_key[32:64], ups[0][1]))
    value = base[32:64, :] + ADAPTER_SCALE * (dot_nt(z_value[0:32], ups[1][0]) + dot_nt(z_value[32:64], ups[1][1]))
    key = (key * cosine + pltpu.roll(key, 64, 1) * sine).astype(BF)
    value = value.astype(BF)
    nk[...] = key.astype(F32)
    nv[...] = value.astype(F32)
    first_step = lax.broadcasted_iota(jnp.int32, (16, 128), 0) < 8
    for r in range(16):
        query = qs[r]
        s0 = jnp.sum(query * nk[r : r + 1, :], axis=1, keepdims=True) * SCALE
        s1 = jnp.sum(query * nk[16 + r : 17 + r, :], axis=1, keepdims=True) * SCALE
        s0 = jnp.broadcast_to(s0, (16, 128))
        s1 = jnp.where(first_step, MASKED, jnp.broadcast_to(s1, (16, 128)))
        top = jnp.maximum(mm[r], jnp.maximum(s0, s1))
        alpha = jnp.exp(mm[r] - top)
        p0 = jnp.exp(s0 - top)
        p1 = jnp.exp(s1 - top)
        total = alpha * ll[r] + p0 + p1
        ctxs[r * 16 : r * 16 + 16, :] = (alpha * acc[r] + p0 * nv[r : r + 1, :] + p1 * nv[16 + r : 17 + r, :]) / total
    for s in range(2):
        for h in range(8):
            ctx[s * 16 : s * 16 + 16, h * 128 : h * 128 + 128] = ctxs[pl.ds(s * 8 + h, 16, stride=16), :].astype(BF)

    context = ctx[...]

    l_w.wait()
    core_peer = tensor_of(1)
    chip_peer = tensor_of(2)

    def part(ref, j):
        return ref.at[:, pl.ds(pl.multiple_of(j * WIDTH, WIDTH), WIDTH)]

    def columns(half, j):
        return pl.ds(pl.multiple_of(half * 2048 + j * WIDTH, WIDTH), WIDTH)

    def give_copy(j):
        return remote(part(ps, j), part(pr, j), pss, prs.at[j], g, core_peer)

    def chip_copy(j):
        return remote(part(ys, j), part(yr, j), yss, yrs.at[j], g, chip_peer)

    def final_copy(j):
        return remote(part(fs, j), att_hbm.at[:, columns(c, j)], fss, frs, g, core_peer)

    def local_copy(j):
        return pltpu.make_async_copy(part(fs, j), att_hbm.at[:, columns(c, j)], outs)

    def give(j, _):
        part(ps, j)[...] = dot(context, w[:, columns(1 - c, j)]).astype(BF)
        give_copy(j).start()
        return 0

    def keep(j, _):
        total = dot(context, w[:, columns(c, j)])
        give_copy(j).wait_recv()
        part(ys, j)[...] = (total + part(pr, j)[...].astype(F32)).astype(BF)
        chip_copy(j).start()
        return 0

    def finish(j, _):
        term = dot(low_sum, part(u, j)[...])
        chip_copy(j).wait_recv()
        part(fs, j)[...] = ((part(ys, j)[...].astype(F32) + part(yr, j)[...].astype(F32)) + term).astype(BF)
        final_copy(j).start()
        local_copy(j).start()
        return 0

    lax.fori_loop(0, 2048 // WIDTH, give, 0)

    keep(0, 0)

    for s in range(2):
        nst[s, 0] = key[s * 16 : s * 16 + 16]
        nst[s, 1] = value[s * 16 : s * 16 + 16]
    l_nkv = pltpu.make_async_copy(nst, nkv_hbm, outk)
    l_nkv.start()

    low = dot(context, dm[...])
    low = low + pltpu.roll(low, 64, 1)
    low = low + pltpu.roll(low, 32, 1)
    lane8 = lax.broadcasted_iota(jnp.int32, (8, 128), 1)
    zos[...] = jnp.where(
        lane8 < 64,
        jnp.where(lane8 < 32, low[0:8], low[8:16]),
        jnp.where(lane8 < 96, low[16:24], low[24:32]),
    )
    for k in (2, 3, 1):
        remote(zos, zor.at[k], os, orr, g, tensor_of(k)).start()

    lax.fori_loop(1, 2048 // WIDTH, keep, 0)

    @pl.when(yh == c)
    def _():
        arrived(gb.at[:, 0:3], b2r)

    @pl.when(yh != c)
    def _():
        arrived(gb, b2r)

    for a in range(16):
        even = gb[a // 2, 2 * (a % 2)].astype(F32)
        odd = gb[a // 2, 2 * (a % 2) + 1].astype(F32)
        u[64:80, a * 128 : a * 128 + 128] = jnp.where(lane16 < 64, even, pltpu.roll(odd, 64, 1)).astype(BF)
        u[80:96, a * 128 : a * 128 + 128] = jnp.where(lane16 < 64, pltpu.roll(even, 64, 1), odd).astype(BF)
    arrived(zor.at[1:4], orr)
    low = (zos[...] + zor[1]) + (zor[2] + zor[3])
    low_sum = jnp.concatenate([pltpu.roll(low, 64, 1), pltpu.roll(low, 32, 1), low, pltpu.roll(low, 96, 1)], axis=0)
    low_sum = jnp.where(jnp.logical_and(lane >= 64, lane < 96), ADAPTER_SCALE * low_sum, 0.0).astype(BF)
    lax.fori_loop(0, 2048 // WIDTH, finish, 0)

    left(r1.at[0:7], a1s)
    left(gt.at[:, 0:7168], a2s)
    left(uo.at[0:7], c2s)
    left(zs, ts)
    left(zor.at[1:4], os)
    left(ps, pss)
    left(ys, yss)
    left(fs, fss)

    @pl.when(yh == c)
    def _():
        left(gb.at[0:7, x], b1s)
        left(gt.at[:, 0:7168], b2s)

    l_nkv.wait()
    pltpu.make_async_copy(fs, fs, outs).wait()
    arrived(fs, frs)


def store(att_in, nkv_in, att_out, nkv_out, sems):
    first = pltpu.make_async_copy(att_in, att_out, sems.at[0])
    second = pltpu.make_async_copy(nkv_in, nkv_out, sems.at[1])
    first.start()
    second.start()
    first.wait()
    second.wait()


def local(hidden, queries, kv_cache, lengths, frozen_key_value, frozen_output_weight, down_kv, up_kv, down_o, up_o):
    hbm = pl.BlockSpec(memory_space=pltpu.HBM)
    dma = pltpu.SemaphoreType.DMA
    args = (
        hidden.reshape(32, 4096),
        queries,
        kv_cache.reshape(32, 256, 128),
        lengths,
        frozen_key_value.reshape(8192, 128),
        frozen_output_weight,
        down_kv.transpose(1, 2, 0).reshape(64, 64),
        up_kv.transpose(0, 2, 3, 1).reshape(2, 2, 32),
        down_o,
        up_o,
    )
    args = tuple(pltpu.with_memory_space_constraint(a, pltpu.HBM) for a in args)
    v = pltpu.VMEM
    attended, new_kv = pl.pallas_call(
        kernel,
        out_shape=(pltpu.VMEM((32, 4096), BF), pltpu.VMEM((2, 2, 16, 128), BF)),
        in_specs=[hbm] * 10,
        out_specs=(hbm, hbm),
        scratch_shapes=[
            v((32, 4096), BF), v((2, 16, 8, 128), BF), v((32, 256, 128), BF), v((8192, 128), BF), v((1024, 4096), BF),
            v((32, 64), BF), v((2, 2, 32), BF), v((8, 2, 32), BF), v((32, 64), BF),
            v((64, 8192), BF), v((16, 16, 128), F32), v((8, 2, 16, 128), BF), v((8, 4, 16, 128), BF),
            v((16, 8192), BF), v((8, 48, 128), BF), v((64, 8192), BF), v((2, 128, 128), BF), v((8, 128, 256), BF), v((1024, 128), BF),
            v((16, 32), F32), v((16, 32), F32),
            v((64, 16), BF), v((64, 16), BF), v((8, 128), F32), v((4, 8, 128), F32),
            v((16, 16, 128), F32), v((16, 16, 128), F32), v((16, 16, 128), F32), v((256, 128), F32),
            v((32, 1024), BF), v((128, 2048), BF),
            v((32, 2048), BF), v((32, 2048), BF), v((32, 2048), BF), v((32, 2048), BF), v((32, 2048), BF),
            v((32, 128), F32), v((32, 128), F32), v((2, 2, 16, 128), BF), v((64, 128), F32), v((16, 16, 256), F32), v((16, 16, 256), BF), pltpu.SMEM((16,), jnp.int32),
            dma((10,)), dma((20,)), dma((2048 // WIDTH,)), dma((2048 // WIDTH,)), dma((8,)),
        ],
        compiler_params=pltpu.CompilerParams(
            collective_id=0, has_side_effects=True, vmem_limit_bytes=40 * 1024 * 1024
        ),
    )(*args)
    attended, new_kv = pl.pallas_call(
        store,
        out_shape=(pltpu.HBM((32, 4096), BF), pltpu.HBM((2, 2, 16, 128), BF)),
        in_specs=[hbm, hbm],
        out_specs=(hbm, hbm),
        scratch_shapes=[dma((2,))],
    )(pltpu.with_memory_space_constraint(attended, pltpu.VMEM), pltpu.with_memory_space_constraint(new_kv, pltpu.VMEM))
    return attended.reshape(2, 16, 4096), new_kv.reshape(2, 2, 16, 1, 128)


def solution(mesh):
    placed = (
        P(None, "group", None),
        P(None, "group", "tensor", None),
        P(None, "group", "tensor", None, None),
        P("group"),
        P(None, None, "tensor"),
        P("tensor", None),
        P("group", None, None),
        P(None, None, "tensor", "group"),
        P("tensor", "group", None),
        P(None, "group"),
    )
    return jax.shard_map(
        local,
        mesh=mesh,
        in_specs=placed,
        out_specs=(P(None, "group", None), P(None, None, "group", "tensor", None)),
        check_vma=False,
    )
```

```python
import math

import jax
import jax.numpy as jnp
from jax import lax
from jax.experimental import pallas as pl
from jax.experimental.pallas import tpu as pltpu
from jax.sharding import PartitionSpec as P

BF = jnp.bfloat16
F32 = jnp.float32
MESH = pl.DeviceIdType.MESH

ADAPTER_SCALE = 2.0
ROPE_BASE = 500000.0
SCALE = 1.0 / math.sqrt(128.0)
MASKED = -1e30
WIDTH = 512

NT = (((1,), (1,)), ((), ()))


def dot(a, b):
    return jnp.dot(a, b, preferred_element_type=F32)


def dot_nt(a, b):
    return lax.dot_general(a, b, NT, preferred_element_type=F32)


def place(rows, columns, offset):
    i = lax.broadcasted_iota(jnp.int32, (rows, columns), 0)
    j = lax.broadcasted_iota(jnp.int32, (rows, columns), 1)
    return jnp.where(j == i + offset, 1.0, 0.0).astype(BF)


def kernel(
    hid_hbm, q_hbm, kv_hbm, len_hbm, fkv_hbm, w_hbm, dkv_hbm, ukv_hbm, do_hbm, uo_hbm,
    att_hbm, nkv_hbm,
    hid, q_v, kv, fkv, w, dk_v, uk_v, do_v, uo_v,
    hx, qs, r1, gb, gt, uo, hd, pu, pm, dm, s16, s4,
    zs, zr, zos, zor, acc, mm, ll, ctxs, ctx, u,
    ps, pr, ys, yr, fs, nk, nv, nst, base, sc, pe, len_ref,
    lsem, one, prs, yrs, came,
):
    a1s, a1r, a2s, a2r, b1s, b1r, b2s, b2r, ts, tr, os, orr, pss, yss, fss, frs, outs, outk, c2s, c2r = (one.at[i] for i in range(20))
    g = lax.axis_index("group")
    t = lax.axis_index("tensor")
    yh = lax.div(g, 32)
    z = lax.rem(lax.div(g, 4), 8)
    x = lax.rem(g, 4)
    yl = lax.div(t, 2)
    c = lax.rem(t, 2)

    def group_of(yh_, z_, x_):
        return yh_ * 32 + z_ * 4 + x_

    def tensor_of(k):
        yl_ = yl if k < 2 else 1 - yl
        c_ = c if k % 2 == 0 else 1 - c
        return yl_ * 2 + c_

    def remote(src, dst, ss, rs, group, tensor):
        return pltpu.make_async_remote_copy(
            src_ref=src, dst_ref=dst, send_sem=ss, recv_sem=rs,
            device_id={"group": group, "tensor": tensor}, device_id_type=MESH,
        )

    barrier = pltpu.get_barrier_semaphore()

    def xy_peer(k):
        return (yh if k < 4 else 1 - yh), lax.rem(x + k % 4, 4)

    def arrived(ref, sem):
        remote(ref, ref, ts, sem, g, t).wait_recv()

    def left(ref, sem):
        remote(ref, ref, sem, tr, g, t).wait_send()

    def load(src, dst, i):
        copy = pltpu.make_async_copy(src, dst, lsem.at[i])
        copy.start()
        return copy

    l_dk = load(dkv_hbm.at[pl.ds(pl.multiple_of(c * 32, 32), 32), :], dk_v, 0)
    l_uk = load(ukv_hbm, uk_v, 1)
    l_do = load(do_hbm, do_v, 2)
    l_uo = load(uo_hbm, uo_v, 3)

    def greet(group, tensor):
        pl.semaphore_signal(barrier, inc=1, device_id={"group": group, "tensor": tensor}, device_id_type=MESH)

    for hop, k in (
        ("xy", 6), ("z", 4), ("z", 3), ("z", 5), ("xy", 5), ("xy", 7), ("xy", 2), ("z", 2), ("z", 6),
        ("xy", 4), ("xy", 1), ("xy", 3), ("z", 1), ("z", 7), ("t", 2), ("t", 3), ("t", 1),
    ):
        if hop == "z":
            greet(group_of(yh, lax.rem(z + k, 8), x), t)
        elif hop == "xy":
            greet(group_of(xy_peer(k)[0], z, xy_peer(k)[1]), t)
        else:
            greet(g, tensor_of(k))

    l_hid = load(hid_hbm, hid, 4)
    l_q = load(q_hbm, q_v, 5)
    l_fkv = load(fkv_hbm, fkv, 6)
    l_kv = load(kv_hbm, kv, 7)
    l_len = load(len_hbm, len_ref, 9)
    l_w = load(w_hbm, w, 8)

    m = lax.rem(z, 4)
    q = lax.rem(m + jnp.where(z < 4, 1, 2), 4)
    l_dk.wait()
    l_uk.wait()
    l_do.wait()
    for h in range(8):
        s16[2 * h : 2 * h + 2, :] = do_v[h].astype(F32)
    for k in range(2):
        for i in range(4):
            s4[4 * i + 2 * k : 4 * i + 2 * k + 2, :] = uk_v[k].astype(F32)
    row16 = lax.broadcasted_iota(jnp.int32, (16, 32), 0)
    up_rows = jnp.where(jnp.logical_and(row16 >= 4 * m, row16 < 4 * m + 4), s4[...], 0.0)
    half = dk_v[...]
    r1[z, 0] = (dot(half[0:16], place(64, 128, 0)) + dot(half[16:32], place(64, 128, 64))).astype(BF)
    r1[z, 1] = (
        dot(s16[...].astype(BF), place(32, 128, 32 * m)) + dot(up_rows.astype(BF), place(32, 128, 32 * q))
    ).astype(BF)
    l_uo.wait()

    @pl.when(yh == c)
    def _():
        up = uo_v[...]
        gb[z, x] = (dot(up[0:16], place(64, 128, 0)) + dot(up[16:32], place(64, 128, 64))).astype(BF)

    lane = lax.broadcasted_iota(jnp.int32, (32, 128), 1)
    pl.semaphore_wait(barrier, 17)

    for k in (4, 3, 5, 2, 6, 1, 7):
        remote(r1.at[z], r1.at[z], a1s, a1r, group_of(yh, lax.rem(z + k, 8), x), t).start()

    feature = lax.broadcasted_iota(jnp.int32, (128, 256), 0)
    source = lax.broadcasted_iota(jnp.int32, (128, 256), 1)

    def digit(value, shift, mask):
        return jnp.bitwise_and(lax.shift_right_logical(value, shift), mask)

    tile = digit(feature, 6, 1) * 4 + digit(feature, 1, 3)
    from_up = (tile * 16 + 4 * digit(feature, 3, 3) + digit(feature, 0, 1))[:, :128]
    from_down = tile * 32 + 16 * digit(feature, 5, 1) + digit(feature, 0, 1)
    for i in range(2):
        pu[i] = jnp.where(source[:, :128] == from_up + 2 * i, 1.0, 0.0).astype(BF)
    for h in range(8):
        pm[h] = jnp.where(source == from_down + 2 * h, 1.0, 0.0).astype(BF)
    square = lax.broadcasted_iota(jnp.int32, (128, 128), 0)
    lane_group = digit(lax.broadcasted_iota(jnp.int32, (128, 128), 1), 5, 3)
    up_lanes = lane_group == digit(digit(square, 3, 3) + 1 + digit(square, 5, 1), 0, 3)
    down_lanes = lane_group == digit(square, 3, 3)

    l_len.wait()
    sub = lax.broadcasted_iota(jnp.int32, (32, 128), 0)
    later = jnp.where(sub >= 16, 1, 0)
    in_step = sub - 16 * later
    position = later
    for r in range(16):
        position = position + jnp.where(in_step == r, len_ref[r], 0)
    counter = jnp.where(lane < 64, lane, lane - 64).astype(F32)
    angle = position.astype(F32) * jnp.exp(counter * (-2.0 * math.log(ROPE_BASE) / 128))
    cosine = jnp.cos(angle)
    sine = jnp.sin(angle)
    sine = jnp.where(lane < 64, -sine, sine)

    l_hid.wait()
    row = lax.broadcasted_iota(jnp.int32, (128, 512), 0)
    col = lax.broadcasted_iota(jnp.int32, (128, 512), 1)
    spread = jnp.where(jnp.where(col < 256, col, col - 257) == 2 * row, 1.0, 0.0).astype(BF)

    def spread_chunk(a, _):
        part = dot(hid[:, pl.ds(pl.multiple_of(a * 128, 128), 128)], spread).astype(BF)
        at = pl.ds(pl.multiple_of(a * 256, 256), 256)
        hx[0:32, at] = part[:, :256]
        hx[32:64, at] = part[:, 256:]
        return 0

    lax.fori_loop(0, 32, spread_chunk, 0, unroll=8)

    for a in range(32):
        pair = hid[:, a * 128 : a * 128 + 128].astype(F32)
        turned = pltpu.roll(pair, 64, 1)
        at = ((a // 16) * 4 + 2 * (a % 2)) * 1024 + (a // 2 % 8) * 128
        hd[0:32, at : at + 128] = jnp.where(lane < 64, pair, 0.0).astype(BF)
        hd[32:64, at : at + 128] = jnp.where(lane < 64, 0.0, turned).astype(BF)
        at = at + 1024
        hd[0:32, at : at + 128] = jnp.where(lane < 64, turned, 0.0).astype(BF)
        hd[32:64, at : at + 128] = jnp.where(lane < 64, 0.0, pair).astype(BF)

    l_fkv.wait()

    def project(a, total):
        at = pl.ds(pl.multiple_of(a * 1024, 1024), 1024)
        return total + dot(hx[:, at], fkv[at, :])

    base[...] = lax.fori_loop(0, 8, project, jnp.zeros((64, 128), F32), unroll=4)

    l_q.wait()
    for s in range(2):
        qs[:, s * 8 : s * 8 + 8, :] = q_v[s].astype(F32)
    l_kv.wait()
    for r in range(16):
        sc[r] = dot_nt(qs[r].astype(BF), kv[r])

    slots = lax.broadcasted_iota(jnp.int32, (16, 256), 1)
    for r in range(16):
        scores = jnp.where(slots < len_ref[r], sc[r] * SCALE, MASKED)
        top = jnp.max(scores, axis=1, keepdims=True)
        expo = jnp.exp(scores - top)
        pe[r] = expo.astype(BF)
        mm[r] = jnp.broadcast_to(top, (16, 128))
        ll[r] = jnp.broadcast_to(jnp.sum(expo, axis=1, keepdims=True), (16, 128))
    for r in range(16):
        acc[r] = dot(pe[r], kv[16 + r])
    u[...] = jnp.zeros_like(u)

    @pl.when(yh == c)
    def _():
        for k in (4, 3, 5, 2, 6, 1, 7):
            remote(gb.at[z, x], gb.at[z, x], b1s, b1r, group_of(yh, lax.rem(z + k, 8), x), t).start()

    lane16 = lax.broadcasted_iota(jnp.int32, (16, 128), 1)
    block = yh * 4 + x
    arrived(r1.at[0:7], a1r)
    for z_ in range(8):
        gt[:, pl.ds(pl.multiple_of(block * 1024 + z_ * 128, 128), 128)] = r1[z_, 0]
    own_lanes = gt.at[:, pl.ds(pl.multiple_of(block * 1024, 1024), 1024)]
    for k in (6, 2, 5, 7, 4, 1, 3):
        yh_, x_ = xy_peer(k)
        remote(own_lanes, own_lanes, a2s, came.at[k], group_of(yh_, z, x_), t).start()
    others = [r1[z_, 1].astype(F32) for z_ in range(8)]

    def lanes_of(z_, i):
        return jnp.where(jnp.logical_and(lane16 >= 32 * i, lane16 < 32 * i + 32), others[z_], 0.0)

    uo[block, 0:16] = sum(lanes_of(z_, (z_ % 4 + 1 + z_ // 4) % 4) for z_ in range(8)).astype(BF)
    uo[block, 16:32] = sum(lanes_of(z_, z_) for z_ in range(4)).astype(BF)
    uo[block, 32:48] = sum(lanes_of(z_, z_ - 4) for z_ in range(4, 8)).astype(BF)
    for k in (6, 2, 5, 7, 4, 1, 3):
        yh_, x_ = xy_peer(k)
        remote(uo.at[block], uo.at[block], c2s, c2r, group_of(yh_, z, x_), t).start()


    def down_part(from_block):
        at = pl.ds(pl.multiple_of(from_block * 1024, 1024), 1024)
        return dot_nt(hd[:, at], gt[:, at])

    low = down_part(block)
    for k in (1, 3, 4, 2, 7, 5, 6):
        from_block = (yh if k < 4 else 1 - yh) * 4 + lax.rem(x + 4 - k % 4, 4)
        arrived(gt.at[:, pl.ds(pl.multiple_of(from_block * 1024, 1024), 1024)], came.at[k])
        low = low + down_part(from_block)
    zs[...] = low.astype(BF)
    remote(zs, zr, ts, tr, g, tensor_of(1)).start()

    @pl.when(yh == c)
    def _():
        arrived(gb.at[0:7, x], b1r)
        for k in (6, 2, 5, 7, 4, 1, 3):
            yh_, x_ = xy_peer(k)
            remote(gb.at[:, x], gb.at[:, x], b2s, b2r, group_of(yh_, z, x_), t).start()

    arrived(uo.at[0:7], c2r)
    gathered = uo[:, 0:16].reshape(128, 128)
    ups = []
    for i in range(2):
        up = jnp.where(up_lanes, dot(pu[i], gathered), 0.0)
        up = up + pltpu.roll(up, 64, 1)
        up = up + pltpu.roll(up, 32, 1)
        ups.append((up[:, 0:16].astype(BF), pltpu.roll(up, 112, 1)[:, 0:16].astype(BF)))
    gathered = uo[:, 16:48].reshape(256, 128)
    for h in range(8):
        dm[h * 128 : h * 128 + 128, :] = jnp.where(down_lanes, dot(pm[h], gathered), 0.0).astype(BF)
    arrived(zr, tr)
    z_key = jnp.where(c == 0, zs[...], zr[...])
    z_value = jnp.where(c == 0, zr[...], zs[...])
    key = base[0:32, :] + ADAPTER_SCALE * (dot_nt(z_key[0:32], ups[0][0]) + dot_nt(z_key[32:64], ups[0][1]))
    value = base[32:64, :] + ADAPTER_SCALE * (dot_nt(z_value[0:32], ups[1][0]) + dot_nt(z_value[32:64], ups[1][1]))
    key = (key * cosine + pltpu.roll(key, 64, 1) * sine).astype(BF)
    value = value.astype(BF)
    nk[...] = key.astype(F32)
    nv[...] = value.astype(F32)
    first_step = lax.broadcasted_iota(jnp.int32, (16, 128), 0) < 8
    for r in range(16):
        query = qs[r]
        s0 = jnp.sum(query * nk[r : r + 1, :], axis=1, keepdims=True) * SCALE
        s1 = jnp.sum(query * nk[16 + r : 17 + r, :], axis=1, keepdims=True) * SCALE
        s0 = jnp.broadcast_to(s0, (16, 128))
        s1 = jnp.where(first_step, MASKED, jnp.broadcast_to(s1, (16, 128)))
        top = jnp.maximum(mm[r], jnp.maximum(s0, s1))
        alpha = jnp.exp(mm[r] - top)
        p0 = jnp.exp(s0 - top)
        p1 = jnp.exp(s1 - top)
        total = alpha * ll[r] + p0 + p1
        ctxs[r * 16 : r * 16 + 16, :] = (alpha * acc[r] + p0 * nv[r : r + 1, :] + p1 * nv[16 + r : 17 + r, :]) / total
    for s in range(2):
        for h in range(8):
            ctx[s * 16 : s * 16 + 16, h * 128 : h * 128 + 128] = ctxs[pl.ds(s * 8 + h, 16, stride=16), :].astype(BF)

    context = ctx[...]

    l_w.wait()
    core_peer = tensor_of(1)
    chip_peer = tensor_of(2)

    def part(ref, j):
        return ref.at[:, pl.ds(pl.multiple_of(j * WIDTH, WIDTH), WIDTH)]

    def columns(half, j):
        return pl.ds(pl.multiple_of(half * 2048 + j * WIDTH, WIDTH), WIDTH)

    def give_copy(j):
        return remote(part(ps, j), part(pr, j), pss, prs.at[j], g, core_peer)

    def chip_copy(j):
        return remote(part(ys, j), part(yr, j), yss, yrs.at[j], g, chip_peer)

    def final_copy(j):
        return remote(part(fs, j), att_hbm.at[:, columns(c, j)], fss, frs, g, core_peer)

    def local_copy(j):
        return pltpu.make_async_copy(part(fs, j), att_hbm.at[:, columns(c, j)], outs)

    def give(j, _):
        part(ps, j)[...] = dot(context, w[:, columns(1 - c, j)]).astype(BF)
        give_copy(j).start()
        return 0

    def keep(j, _):
        total = dot(context, w[:, columns(c, j)])
        give_copy(j).wait_recv()
        part(ys, j)[...] = (total + part(pr, j)[...].astype(F32)).astype(BF)
        chip_copy(j).start()
        return 0

    def finish(j, _):
        term = dot(low_sum, part(u, j)[...])
        chip_copy(j).wait_recv()
        part(fs, j)[...] = ((part(ys, j)[...].astype(F32) + part(yr, j)[...].astype(F32)) + term).astype(BF)
        final_copy(j).start()
        local_copy(j).start()
        return 0

    lax.fori_loop(0, 2048 // WIDTH, give, 0)

    keep(0, 0)

    for s in range(2):
        nst[s, 0] = key[s * 16 : s * 16 + 16]
        nst[s, 1] = value[s * 16 : s * 16 + 16]
    l_nkv = pltpu.make_async_copy(nst, nkv_hbm, outk)
    l_nkv.start()

    low = dot(context, dm[...])
    low = low + pltpu.roll(low, 64, 1)
    low = low + pltpu.roll(low, 32, 1)
    lane8 = lax.broadcasted_iota(jnp.int32, (8, 128), 1)
    zos[...] = jnp.where(
        lane8 < 64,
        jnp.where(lane8 < 32, low[0:8], low[8:16]),
        jnp.where(lane8 < 96, low[16:24], low[24:32]),
    )
    for k in (2, 3, 1):
        remote(zos, zor.at[k], os, orr, g, tensor_of(k)).start()

    lax.fori_loop(1, 2048 // WIDTH, keep, 0)

    @pl.when(yh == c)
    def _():
        arrived(gb.at[:, 0:3], b2r)

    @pl.when(yh != c)
    def _():
        arrived(gb, b2r)

    for a in range(16):
        even = gb[a // 2, 2 * (a % 2)].astype(F32)
        odd = gb[a // 2, 2 * (a % 2) + 1].astype(F32)
        u[64:80, a * 128 : a * 128 + 128] = jnp.where(lane16 < 64, even, pltpu.roll(odd, 64, 1)).astype(BF)
        u[80:96, a * 128 : a * 128 + 128] = jnp.where(lane16 < 64, pltpu.roll(even, 64, 1), odd).astype(BF)
    arrived(zor.at[1:4], orr)
    low = (zos[...] + zor[1]) + (zor[2] + zor[3])
    low_sum = jnp.concatenate([pltpu.roll(low, 64, 1), pltpu.roll(low, 32, 1), low, pltpu.roll(low, 96, 1)], axis=0)
    low_sum = jnp.where(jnp.logical_and(lane >= 64, lane < 96), ADAPTER_SCALE * low_sum, 0.0).astype(BF)
    lax.fori_loop(0, 2048 // WIDTH, finish, 0)

    left(r1.at[0:7], a1s)
    left(gt.at[:, 0:7168], a2s)
    left(uo.at[0:7], c2s)
    left(zs, ts)
    left(zor.at[1:4], os)
    left(ps, pss)
    left(ys, yss)
    left(fs, fss)

    @pl.when(yh == c)
    def _():
        left(gb.at[0:7, x], b1s)
        left(gt.at[:, 0:7168], b2s)

    l_nkv.wait()
    pltpu.make_async_copy(fs, fs, outs).wait()
    arrived(fs, frs)


def store(att_in, nkv_in, att_out, nkv_out, sems):
    first = pltpu.make_async_copy(att_in, att_out, sems.at[0])
    second = pltpu.make_async_copy(nkv_in, nkv_out, sems.at[1])
    first.start()
    second.start()
    first.wait()
    second.wait()


def local(hidden, queries, kv_cache, lengths, frozen_key_value, frozen_output_weight, down_kv, up_kv, down_o, up_o):
    hbm = pl.BlockSpec(memory_space=pltpu.HBM)
    dma = pltpu.SemaphoreType.DMA
    args = (
        hidden.reshape(32, 4096),
        queries,
        kv_cache.reshape(32, 256, 128),
        lengths,
        frozen_key_value.reshape(8192, 128),
        frozen_output_weight,
        down_kv.transpose(1, 2, 0).reshape(64, 64),
        up_kv.transpose(0, 2, 3, 1).reshape(2, 2, 32),
        down_o,
        up_o,
    )
    args = tuple(pltpu.with_memory_space_constraint(a, pltpu.HBM) for a in args)
    v = pltpu.VMEM
    attended, new_kv = pl.pallas_call(
        kernel,
        out_shape=(pltpu.VMEM((32, 4096), BF), pltpu.VMEM((2, 2, 16, 128), BF)),
        in_specs=[hbm] * 10,
        out_specs=(hbm, hbm),
        scratch_shapes=[
            v((32, 4096), BF), v((2, 16, 8, 128), BF), v((32, 256, 128), BF), v((8192, 128), BF), v((1024, 4096), BF),
            v((32, 64), BF), v((2, 2, 32), BF), v((8, 2, 32), BF), v((32, 64), BF),
            v((64, 8192), BF), v((16, 16, 128), F32), v((8, 2, 16, 128), BF), v((8, 4, 16, 128), BF),
            v((16, 8192), BF), v((8, 48, 128), BF), v((64, 8192), BF), v((2, 128, 128), BF), v((8, 128, 256), BF), v((1024, 128), BF),
            v((16, 32), F32), v((16, 32), F32),
            v((64, 16), BF), v((64, 16), BF), v((8, 128), F32), v((4, 8, 128), F32),
            v((16, 16, 128), F32), v((16, 16, 128), F32), v((16, 16, 128), F32), v((256, 128), F32),
            v((32, 1024), BF), v((128, 2048), BF),
            v((32, 2048), BF), v((32, 2048), BF), v((32, 2048), BF), v((32, 2048), BF), v((32, 2048), BF),
            v((32, 128), F32), v((32, 128), F32), v((2, 2, 16, 128), BF), v((64, 128), F32), v((16, 16, 256), F32), v((16, 16, 256), BF), pltpu.SMEM((16,), jnp.int32),
            dma((10,)), dma((20,)), dma((2048 // WIDTH,)), dma((2048 // WIDTH,)), dma((8,)),
        ],
        compiler_params=pltpu.CompilerParams(
            collective_id=0, has_side_effects=True, vmem_limit_bytes=40 * 1024 * 1024
        ),
    )(*args)
    attended, new_kv = pl.pallas_call(
        store,
        out_shape=(pltpu.HBM((32, 4096), BF), pltpu.HBM((2, 2, 16, 128), BF)),
        in_specs=[hbm, hbm],
        out_specs=(hbm, hbm),
        scratch_shapes=[dma((2,))],
    )(pltpu.with_memory_space_constraint(attended, pltpu.VMEM), pltpu.with_memory_space_constraint(new_kv, pltpu.VMEM))
    return attended.reshape(2, 16, 4096), new_kv.reshape(2, 2, 16, 1, 128)


def solution(mesh):
    placed = (
        P(None, "group", None),
        P(None, "group", "tensor", None),
        P(None, "group", "tensor", None, None),
        P("group"),
        P(None, None, "tensor"),
        P("tensor", None),
        P("group", None, None),
        P(None, None, "tensor", "group"),
        P("tensor", "group", None),
        P(None, "group"),
    )
    return jax.shard_map(
        local,
        mesh=mesh,
        in_specs=placed,
        out_specs=(P(None, "group", None), P(None, None, "group", "tensor", None)),
        check_vma=False,
    )
```
